128 devices in a mesh: lat: 2 (over x_lo), lon: 64 (over x_hi, z, y, core).
Axes of the slice: x: 4 (x_hi: 2, x_lo: 2; x = x_hi * 2 + x_lo), y: 4, z: 4, core: 2. Of those that a mesh axis runs over, the one named last changes fastest.
Arguments:
- fields: bfloat16 [16, 4096, 512], P('lat', 'lon'), may hold values from -6 to 6
- surface: int32 [16, 4096], P('lat', 'lon'), may hold values from 0 to 2
- surface_table: float32 [3, 512], replicated, may hold values from -4 to 4
- logit_scale: float32 [8], replicated, may hold values from 2 to 12
- w_qkv: bfloat16 [512, 1536], replicated, may hold values from -0.25 to 0.25
- w_out: bfloat16 [512, 512], replicated, may hold values from -0.25 to 0.25
- w_merge: bfloat16 [2048, 1024], P(('lat', 'lon')), may hold values from -0.125 to 0.125
- w_split: bfloat16 [1024, 2048], P(('lat', 'lon')), may hold values from -0.1875 to 0.1875
- cotangent: bfloat16 [16, 4096, 512], P('lat', 'lon'), may hold values from -6 to 6
Outputs:
- decoded: bfloat16 [16, 4096, 512], P('lat', 'lon')
- grad_fields: bfloat16 [16, 4096, 512], P('lat', 'lon')
- grad_qkv_weight: float32 [512, 1536], P(('lat', 'lon'))
- grad_out_weight: float32 [512, 512], P(('lat', 'lon'))
- grad_merge_weight: float32 [2048, 1024], P(('lat', 'lon'))
- grad_split_weight: float32 [1024, 2048], P(('lat', 'lon'))
The draws below stay inside these ranges and needn't reach their ends.
All inputs are finite; a program needn't handle non-finite values.
Results may differ from the reference program's by a relative error of at most 0.017.
Values may be sent and summed in bfloat16 or wider, within the bound.
No kernel may reach another device: no remote copies, remote signals or barrier semaphores. Data moves between devices by JAX's collectives and lax.ppermute only.
A program may use at most 128 MiB of HBM per device.

```python
import math
import jax
import jax.numpy as jnp
from jax import lax

D = 512
DC = 1024
HEADS = 8
WIN = 8
SHIFT = 4
NLAT = 16
NLON = 4096


def set_ends(entries, key, smallest, largest):
    spot = [jax.random.randint(jax.random.fold_in(key, axis), (), 0, length) for axis, length in enumerate(entries.shape)]
    widest = entries.shape.index(max(entries.shape))
    neighbour = spot[:widest] + [(spot[widest] + 1) % entries.shape[widest]] + spot[widest + 1:]
    return entries.at[tuple(spot)].set(smallest).at[tuple(neighbour)].set(largest)


def shard_levels(rng, extent, cuts, smallest, high):
    level = 1.0
    for position, parts in cuts:
        steps = jax.random.uniform(jax.random.fold_in(jax.random.fold_in(rng, 6), position), (parts,), jnp.float32, smallest / len(cuts), high / len(cuts))
        level = level * jnp.repeat(jnp.exp(steps), extent[position] // parts).reshape((-1,) + (1,) * (len(extent) - 1 - position))
    return level


def centred(key, extent, scale, reach, split=(), kind=jnp.bfloat16):
    gain = shard_levels(key, extent, split, -0.22, 0.18) if split else 1.0
    values = jax.random.normal(key, extent, jnp.float32) * scale * gain
    return jnp.minimum(jnp.maximum(values, -reach), reach).astype(kind)


def setup_inputs(seed: int = 0) -> dict:
    splits = jax.random.split(jax.random.key(seed), 10)
    fields = centred(splits[0], (NLAT, NLON, D), 1.0, 6.0, ((0, 2), (1, 64)))
    surface = set_ends(jax.random.randint(splits[1], (NLAT, NLON), 0, 3), jax.random.fold_in(splits[1], 1), 0, 2).astype(jnp.int32)
    surface_table = centred(splits[2], (3, D), 1.0, 4.0, (), jnp.float32)
    logit_scale = jnp.clip(jnp.exp(jax.random.uniform(splits[3], (HEADS,), jnp.float32, math.log(2.0), math.log(12.0))), 2.0, 12.0)
    w_qkv = centred(splits[4], (D, 3 * D), D ** -0.5, 0.25)
    w_out = centred(splits[5], (D, D), D ** -0.5, 0.25)
    w_merge = centred(splits[6], (4 * D, DC), (4 * D) ** -0.5, 0.125, ((0, 128),))
    w_split = centred(splits[7], (DC, 4 * D), DC ** -0.5, 0.1875, ((0, 128),))
    cotangent = centred(splits[8], (NLAT, NLON, D), 1.0, 6.0, ((0, 2), (1, 64)))
    return {"fields": fields, "surface": surface, "surface_table": surface_table, "logit_scale": logit_scale, "w_qkv": w_qkv, "w_out": w_out, "w_merge": w_merge, "w_split": w_split, "cotangent": cotangent}


EPS_NORM = 1e-05
EPS_UNIT = 1e-06

def layer_norm(values):
    centre = values - lax.optimization_barrier(jnp.mean(values, axis=-1, keepdims=True))
    spread = lax.optimization_barrier(jnp.mean(centre * centre, axis=-1, keepdims=True))
    return centre * lax.rsqrt(spread + EPS_NORM)

def rounded_norm(values):
    return layer_norm(values).astype(jnp.bfloat16)

def inner(left, right):
    return lax.dot_general(left, right, (((0,), (0,)), ((), ())), preferred_element_type=jnp.float32)

def merge_cells(grid):
    lat_rows, lon_cols, feat_count = grid.shape
    blocks = grid.reshape(lat_rows // 2, 2, lon_cols // 2, 2, feat_count).transpose(0, 2, 1, 3, 4)
    return blocks.reshape(lat_rows * lon_cols // 4, 4 * feat_count)

def split_cells(flat, lat_rows, lon_cols):
    feat_count = flat.shape[1] // 4
    blocks = flat.reshape(lat_rows // 2, lon_cols // 2, 2, 2, feat_count).transpose(0, 2, 1, 3, 4)
    return blocks.reshape(lat_rows, lon_cols, feat_count)

def window_attention(packed, region, logit_scale):
    grid_rows, grid_cols, triple_width = packed.shape
    model_width = triple_width // 3
    head_size = model_width // HEADS
    win_rows = grid_rows // WIN
    win_cols = grid_cols // WIN
    windows = packed.reshape(win_rows, WIN, win_cols, WIN, 3, HEADS, head_size)
    windows = windows.transpose(0, 2, 1, 3, 4, 5, 6).reshape(win_rows * win_cols, WIN * WIN, 3, HEADS, head_size)
    queries = windows[:, :, 0]
    key_rows = windows[:, :, 1]
    values = windows[:, :, 2].astype(jnp.bfloat16)
    query_unit = (queries * lax.rsqrt(lax.optimization_barrier(jnp.sum(queries * queries, axis=-1, keepdims=True)) + EPS_UNIT)).astype(jnp.bfloat16)
    key_unit = (key_rows * lax.rsqrt(lax.optimization_barrier(jnp.sum(key_rows * key_rows, axis=-1, keepdims=True)) + EPS_UNIT)).astype(jnp.bfloat16)
    scores = jnp.einsum('wqhd,wkhd->whqk', query_unit.astype(jnp.float32), key_unit.astype(jnp.float32))
    scores = scores * logit_scale[None, :, None, None]
    labels = jnp.broadcast_to(region.reshape(win_rows, 1, WIN, 1), (win_rows, win_cols, WIN, WIN))
    labels = labels.reshape(win_rows * win_cols, WIN * WIN)
    same_region = labels[:, :, None] == labels[:, None, :]
    exponent = jnp.where(same_region[:, None], jnp.exp(scores), jnp.float32(0.0))
    weights = (exponent / lax.optimization_barrier(jnp.sum(exponent, axis=-1, keepdims=True))).astype(jnp.bfloat16)
    attended = jnp.einsum('whqk,wkhd->wqhd', weights.astype(jnp.float32), values.astype(jnp.float32)).astype(jnp.bfloat16)
    attended = attended.reshape(win_rows, win_cols, WIN, WIN, model_width).transpose(0, 2, 1, 3, 4)
    return attended.reshape(grid_rows, grid_cols, model_width)

def reference(fields, surface, surface_table, logit_scale, w_qkv, w_out, w_merge, w_split, cotangent):
    classes = (surface[:, :, None] == jnp.arange(3, dtype=jnp.int32)).astype(jnp.float32)
    table_rows = jnp.dot(classes.reshape(-1, 3), surface_table, precision=lax.Precision.HIGHEST)
    embedded = fields.astype(jnp.float32) + table_rows.reshape(NLAT, NLON, D)
    normed, normed_back = jax.vjp(rounded_norm, embedded)
    shifted = jnp.roll(normed, (-SHIFT, -SHIFT), (0, 1))
    region = (jnp.arange(NLAT) >= NLAT - SHIFT).astype(jnp.int32)
    block_count = NLAT // WIN
    shifted_blocks = shifted.reshape(block_count, WIN, NLON, D)
    region_blocks = region.reshape(block_count, WIN)

    def forward_block(inputs):
        block, labels = inputs
        packed = jnp.dot(block.reshape(-1, D), w_qkv, preferred_element_type=jnp.float32).reshape(WIN, NLON, 3 * D)
        attended = window_attention(packed, labels, logit_scale)
        projected = jnp.dot(attended.reshape(-1, D), w_out, preferred_element_type=jnp.float32)
        return projected.astype(jnp.bfloat16).reshape(WIN, NLON, D)
    projected = lax.map(forward_block, (shifted_blocks, region_blocks)).reshape(NLAT, NLON, D)
    skip = (embedded + jnp.roll(projected, (SHIFT, SHIFT), (0, 1)).astype(jnp.float32)).astype(jnp.bfloat16)
    merged = merge_cells(skip)
    merged_norm, norm_back = jax.vjp(rounded_norm, merged.astype(jnp.float32))
    coarse_pre = jnp.dot(merged_norm, w_merge, preferred_element_type=jnp.float32)
    coarse_full, gelu_back = jax.vjp(jax.nn.gelu, coarse_pre)
    coarse = coarse_full.astype(jnp.bfloat16)
    split_out = jnp.dot(coarse, w_split, preferred_element_type=jnp.float32)
    decoded = (skip.astype(jnp.float32) + split_cells(split_out, NLAT, NLON)).astype(jnp.bfloat16)
    merged_cot = merge_cells(cotangent)
    grad_split = inner(coarse, merged_cot)
    grad_coarse = jnp.dot(merged_cot, w_split.T, preferred_element_type=jnp.float32)
    grad_pre = gelu_back(grad_coarse)[0].astype(jnp.bfloat16)
    grad_merge = inner(merged_norm, grad_pre)
    grad_mnorm = jnp.dot(grad_pre, w_merge.T, preferred_element_type=jnp.float32).astype(jnp.bfloat16)
    grad_skip = cotangent.astype(jnp.float32) + split_cells(norm_back(grad_mnorm)[0], NLAT, NLON)
    grad_shifted = jnp.roll(grad_skip.astype(jnp.bfloat16), (-SHIFT, -SHIFT), (0, 1))

    def backward_block(carry, inputs):
        grad_qkv_sum, grad_out_sum = carry
        block, labels, grad_block = inputs
        flat_block = block.reshape(-1, D)
        packed = jnp.dot(flat_block, w_qkv, preferred_element_type=jnp.float32).reshape(WIN, NLON, 3 * D)
        attended, attend_back = jax.vjp(lambda packed_qkv: window_attention(packed_qkv, labels, logit_scale), packed)
        flat_grad = grad_block.reshape(-1, D)
        grad_att = jnp.dot(flat_grad, w_out.T, preferred_element_type=jnp.float32).astype(jnp.bfloat16)
        grad_packed = attend_back(grad_att.reshape(WIN, NLON, D))[0].reshape(-1, 3 * D).astype(jnp.bfloat16)
        grad_qkv_sum = grad_qkv_sum + inner(flat_block, grad_packed)
        grad_out_sum = grad_out_sum + inner(attended.reshape(-1, D), flat_grad)
        grad_normed = jnp.dot(grad_packed, w_qkv.T, preferred_element_type=jnp.float32).astype(jnp.bfloat16)
        return ((grad_qkv_sum, grad_out_sum), grad_normed.reshape(WIN, NLON, D))
    start_sums = (jnp.zeros((D, 3 * D), jnp.float32), jnp.zeros((D, D), jnp.float32))
    grad_inputs = (shifted_blocks, region_blocks, grad_shifted.reshape(block_count, WIN, NLON, D))
    (grad_qkv_weight, grad_out_weight), grad_blocks = lax.scan(backward_block, start_sums, grad_inputs)
    grad_normed = jnp.roll(grad_blocks.reshape(NLAT, NLON, D), (SHIFT, SHIFT), (0, 1))
    grad_fields = (grad_skip + normed_back(grad_normed)[0]).astype(jnp.bfloat16)
    return (decoded, grad_fields, grad_qkv_weight, grad_out_weight, grad_merge, grad_split)
```

```python
import jax
import jax.numpy as jnp
from jax import lax
from jax.sharding import Mesh, PartitionSpec as P

HEADS = 8
WIN = 8
SHIFT = 4


EPS_NORM = 1e-05
EPS_UNIT = 1e-06


LON = ("xh", "z", "y", "c")


def from_behind(value, axis, steps):
    name = "xl" if axis == "lat" else LON
    count = 2 if axis == "lat" else 64
    pairs = [(source, (source + steps) % count) for source in range(count)]
    return lax.ppermute(value, name, pairs)


AXES = ("xl", "xh", "z", "y", "c")
CHIP_AXES = ("xl", "xh", "z", "y")


def places():
    return {
        "x": 2 * lax.axis_index("xh") + lax.axis_index("xl"),
        "y": lax.axis_index("y"),
        "z": lax.axis_index("z"),
        "c": lax.axis_index("c"),
    }


def device_index(x, y, z, c):
    return ((((x % 2) * 2 + x // 2) * 4 + z) * 4 + y) * 2 + c


def move(value, x=0, y=0, z=0, c=0):
    pairs = []
    for px in range(4):
        for pz in range(4):
            for py in range(4):
                for pc in range(2):
                    target = ((px + x) % 4, (py + y) % 4, (pz + z) % 4, (pc + c) % 2)
                    pairs.append((device_index(px, py, pz, pc), device_index(*target)))
    return lax.ppermute(value, AXES, pairs)


def slot_of(axis, place):
    return (place % 2) * 2 + place // 2 if axis == "x" else place


def gather_ring(block, axis, place):
    ahead = move(block, **{axis: -1})
    behind = move(block, **{axis: 1})
    across = move(block, **{axis: 2})
    ring = jnp.zeros((4,) + block.shape, block.dtype)
    for offset, part in ((0, block), (1, ahead), (2, across), (3, behind)):
        ring = lax.dynamic_update_index_in_dim(ring, part, slot_of(axis, (place + offset) % 4), 0)
    return ring


def scatter_ring(blocks, axis, place, dim):
    def block_for(offset):
        return lax.dynamic_index_in_dim(
            blocks, slot_of(axis, (place + offset) % 4), dim, keepdims=False
        )

    ahead = move(block_for(1), **{axis: 1})
    behind = move(block_for(3), **{axis: -1})
    across = move(block_for(2), **{axis: 2})
    total = block_for(0).astype(jnp.float32) + ahead.astype(jnp.float32)
    return total + behind.astype(jnp.float32) + across.astype(jnp.float32)


def half_of(value, which):
    width = value.shape[-1] // 2
    return lax.dynamic_slice_in_dim(value, which * width, width, value.ndim - 1)


def join_cores(mine, other, core, axis):
    return jnp.where(
        core == 0,
        jnp.concatenate([mine, other], axis=axis),
        jnp.concatenate([other, mine], axis=axis),
    )


def gather_weight(shard, order, place):
    core = place["c"]
    swapped = move(half_of(shard, 1 - core), c=1)
    block = join_cores(half_of(shard, core), swapped, core, 0)
    rows, cols = block.shape
    digits = []
    for axis in order:
        block = gather_ring(block, axis, place[axis])
        digits.insert(0, axis)
    spots = [digits.index(axis) for axis in ("x", "z", "y")]
    block = block.transpose(spots + [3, 4]).reshape(64 * rows, cols)
    other = move(block, c=1)
    return join_cores(block, other, core, 1)


def scatter_half(half, order, place):
    rows, cols = half.shape
    blocks = half.astype(jnp.bfloat16).reshape(4, 4, 4, rows // 64, cols)
    digits = ["x", "z", "y"]
    for axis in order:
        blocks = scatter_ring(blocks, axis, place[axis], digits.index(axis))
        digits.remove(axis)
        if digits:
            blocks = blocks.astype(jnp.bfloat16)
    return own_rows(blocks, place["c"])


def own_rows(block, core):
    rows = block.shape[0] // 2
    mine = lax.dynamic_slice_in_dim(block, core * rows, rows, 0)
    other = move(lax.dynamic_slice_in_dim(block, (1 - core) * rows, rows, 0), c=1)
    return join_cores(mine, other, core, 1)


def pair_inner(left, right, core):
    left_other = move(left, c=1)
    right_other = move(half_of(right, 1 - core), c=1)
    return inner(
        jnp.concatenate([left, left_other], axis=0),
        jnp.concatenate([half_of(right, core), right_other], axis=0),
    )


def layer_norm(values):
    centre = values - jnp.mean(values, axis=-1, keepdims=True)
    spread = jnp.mean(centre * centre, axis=-1, keepdims=True)
    return centre * lax.rsqrt(spread + EPS_NORM)


def rounded_norm(values):
    return layer_norm(values).astype(jnp.bfloat16)


def inner(left, right):
    return lax.dot_general(
        left, right, (((0,), (0,)), ((), ())), preferred_element_type=jnp.float32
    )


def merge_cells(grid):
    lat_rows, lon_cols, feat_count = grid.shape
    blocks = grid.reshape(lat_rows // 2, 2, lon_cols // 2, 2, feat_count).transpose(0, 2, 1, 3, 4)
    return blocks.reshape(lat_rows * lon_cols // 4, 4 * feat_count)


def split_cells(flat, lat_rows, lon_cols):
    feat_count = flat.shape[1] // 4
    blocks = flat.reshape(lat_rows // 2, lon_cols // 2, 2, 2, feat_count).transpose(0, 2, 1, 3, 4)
    return blocks.reshape(lat_rows, lon_cols, feat_count)


def window_attention(packed, region, logit_scale):
    grid_rows, grid_cols, triple_width = packed.shape
    model_width = triple_width // 3
    head_size = model_width // HEADS
    win_rows = grid_rows // WIN
    win_cols = grid_cols // WIN
    windows = packed.reshape(win_rows, WIN, win_cols, WIN, 3, HEADS, head_size)
    windows = windows.transpose(0, 2, 1, 3, 4, 5, 6).reshape(
        win_rows * win_cols, WIN * WIN, 3, HEADS, head_size
    )
    queries = windows[:, :, 0]
    key_rows = windows[:, :, 1]
    values = windows[:, :, 2].astype(jnp.bfloat16)
    query_unit = (
        queries * lax.rsqrt(jnp.sum(queries * queries, axis=-1, keepdims=True) + EPS_UNIT)
    ).astype(jnp.bfloat16)
    key_unit = (
        key_rows * lax.rsqrt(jnp.sum(key_rows * key_rows, axis=-1, keepdims=True) + EPS_UNIT)
    ).astype(jnp.bfloat16)
    scores = jnp.einsum("wqhd,wkhd->whqk", query_unit, key_unit, preferred_element_type=jnp.float32)
    scores = scores * logit_scale[None, :, None, None]
    labels = jnp.broadcast_to(region.reshape(win_rows, 1, WIN, 1), (win_rows, win_cols, WIN, WIN))
    labels = labels.reshape(win_rows * win_cols, WIN * WIN)
    same_region = labels[:, :, None] == labels[:, None, :]
    exponent = jnp.where(same_region[:, None], jnp.exp(scores), jnp.float32(0.0))
    weights = (exponent / jnp.sum(exponent, axis=-1, keepdims=True)).astype(jnp.bfloat16)
    attended = jnp.einsum(
        "whqk,wkhd->wqhd", weights, values, preferred_element_type=jnp.float32
    ).astype(jnp.bfloat16)
    attended = attended.reshape(win_rows, win_cols, WIN, WIN, model_width).transpose(0, 2, 1, 3, 4)
    return attended.reshape(grid_rows, grid_cols, model_width)


def fetch_rim(field):
    top_strip = from_behind(field[:SHIFT], "lat", -1)
    side_strip = from_behind(field[:, :SHIFT], "lon", -1)
    corner = from_behind(side_strip[:SHIFT], "lat", -1)
    upper = jnp.concatenate([field[SHIFT:, SHIFT:], side_strip[SHIFT:]], axis=1)
    lower = jnp.concatenate([top_strip[:, SHIFT:], corner], axis=1)
    return jnp.concatenate([upper, lower], axis=0)


def return_rim(shifted):
    side_back = from_behind(shifted[:, -SHIFT:], "lon", 1)
    top_back = from_behind(shifted[-SHIFT:, :-SHIFT], "lat", 1)
    corner = from_behind(side_back[-SHIFT:], "lat", 1)
    upper = jnp.concatenate([corner, top_back], axis=1)
    lower = jnp.concatenate([side_back[:-SHIFT], shifted[:-SHIFT, :-SHIFT]], axis=1)
    return jnp.concatenate([upper, lower], axis=0)


def per_device(
    fields, surface, surface_table, logit_scale, w_qkv, w_out, w_merge, w_split, cotangent
):
    lat_rows, lon_cols, model_width = fields.shape
    token_count = lat_rows * lon_cols
    place = places()
    core = place["c"]
    split_full = gather_weight(w_split, ("y", "x", "z"), place)
    merge_full = gather_weight(w_merge, ("z", "y", "x"), place)
    classes = (surface[:, :, None] == jnp.arange(3, dtype=jnp.int32)).astype(jnp.float32)
    table_rows = jnp.dot(classes.reshape(-1, 3), surface_table, precision=lax.Precision.HIGHEST)
    embedded = fields.astype(jnp.float32) + table_rows.reshape(lat_rows, lon_cols, model_width)
    normed, normed_back = jax.vjp(rounded_norm, embedded)
    shifted = fetch_rim(normed)
    flat_shifted = shifted.reshape(token_count, model_width)
    packed = jnp.dot(flat_shifted, w_qkv, preferred_element_type=jnp.float32).reshape(
        lat_rows, lon_cols, 3 * model_width
    )
    row_index = lax.axis_index("xl") * lat_rows + jnp.arange(lat_rows, dtype=jnp.int32)
    region = (row_index >= lat_rows * lax.axis_size("xl") - SHIFT).astype(jnp.int32)
    attended, attend_back = jax.vjp(
        lambda packed_qkv: window_attention(packed_qkv, region, logit_scale), packed
    )
    flat_att = attended.reshape(token_count, model_width)
    projected = jnp.dot(flat_att, w_out, preferred_element_type=jnp.float32).astype(jnp.bfloat16)
    projected = projected.reshape(lat_rows, lon_cols, model_width)
    skip = (embedded + return_rim(projected).astype(jnp.float32)).astype(jnp.bfloat16)
    merged = merge_cells(skip)
    merged_norm, norm_back = jax.vjp(rounded_norm, merged.astype(jnp.float32))
    coarse_pre = jnp.dot(merged_norm, merge_full, preferred_element_type=jnp.float32)
    coarse_full, gelu_back = jax.vjp(jax.nn.gelu, coarse_pre)
    coarse = coarse_full.astype(jnp.bfloat16)
    split_out = jnp.dot(coarse, split_full, preferred_element_type=jnp.float32)
    decoded = (skip.astype(jnp.float32) + split_cells(split_out, lat_rows, lon_cols)).astype(
        jnp.bfloat16
    )
    merged_cot = merge_cells(cotangent)
    grad_coarse = jnp.dot(merged_cot, split_full.T, preferred_element_type=jnp.float32)
    grad_pre = gelu_back(grad_coarse)[0].astype(jnp.bfloat16)
    grad_mnorm = jnp.dot(grad_pre, merge_full.T, preferred_element_type=jnp.float32).astype(
        jnp.bfloat16
    )
    grad_skip = cotangent.astype(jnp.float32) + split_cells(
        norm_back(grad_mnorm)[0], lat_rows, lon_cols
    )
    grad_shifted = fetch_rim(grad_skip.astype(jnp.bfloat16))
    flat_grad = grad_shifted.reshape(token_count, model_width)
    grad_att = jnp.dot(flat_grad, w_out.T, preferred_element_type=jnp.float32).astype(jnp.bfloat16)
    grad_packed = attend_back(grad_att.reshape(lat_rows, lon_cols, model_width))[0]
    grad_packed = grad_packed.reshape(token_count, 3 * model_width).astype(jnp.bfloat16)
    grad_split = scatter_half(pair_inner(coarse, merged_cot, core), ("x", "z", "y"), place)
    grad_merge = scatter_half(pair_inner(merged_norm, grad_pre, core), ("z", "y", "x"), place)
    qkv_part = inner(flat_shifted, grad_packed)
    out_part = inner(flat_att, flat_grad)
    fine_part = jnp.concatenate([qkv_part, out_part], axis=1).astype(jnp.bfloat16)
    fine_other = move(half_of(fine_part, 1 - core), c=1)
    fine_half = half_of(fine_part, core).astype(jnp.float32) + fine_other.astype(jnp.float32)
    fine_blocks = lax.all_to_all(fine_half.astype(jnp.bfloat16), CHIP_AXES, 0, 0, tiled=True)
    fine_sum = jnp.sum(fine_blocks.astype(jnp.float32).reshape(64, model_width // 64, -1), axis=0)
    fine_grads = own_rows(fine_sum, core)
    grad_qkv_weight = fine_grads[:, : 3 * model_width]
    grad_out_weight = fine_grads[:, 3 * model_width :]
    grad_normed = jnp.dot(grad_packed, w_qkv.T, preferred_element_type=jnp.float32).astype(
        jnp.bfloat16
    )
    grad_normed = return_rim(grad_normed.reshape(lat_rows, lon_cols, model_width))
    grad_fields = (grad_skip + normed_back(grad_normed)[0]).astype(jnp.bfloat16)
    return (decoded, grad_fields, grad_qkv_weight, grad_out_weight, grad_merge, grad_split)


def solution(mesh):
    fine_mesh = Mesh(mesh.devices.reshape(2, 2, 4, 4, 2), AXES)
    grid, rows = P("xl", LON, None), P(AXES, None)
    in_specs = (grid, P("xl", LON), P(), P(), P(), P(), rows, rows, grid)
    out_specs = (grid, grid, rows, rows, rows, rows)
    return jax.shard_map(
        per_device, mesh=fine_mesh, in_specs=in_specs, out_specs=out_specs, check_vma=False
    )
```

```python
import functools

import jax
import jax.numpy as jnp
from jax import lax
from jax.experimental import pallas as pl
from jax.experimental.pallas import tpu as pltpu
from jax.sharding import Mesh, PartitionSpec as P

HEADS = 8
WIN = 8
SHIFT = 4
EPS_NORM = 1e-05
EPS_UNIT = 1e-06

D = 512
ROWS, COLS = 8, 64
WINS = COLS // WIN + 1
CELLS = 24
OWN = 16
PATCHES = 4 * CELLS
TOKENS = WINS * PATCHES
ALL_CELLS = WINS * CELLS
OWN_CELLS = WINS * OWN
LANES = 128
VMEM_BYTES = 48 * 1024 * 1024

AXES = ("xl", "xh", "z", "y", "c")
CHIP_AXES = ("xl", "xh", "z", "y")
LON = ("xh", "z", "y", "c")

F32 = jnp.float32
BF16 = jnp.bfloat16


def device_index(x, y, z, c):
    return ((((x % 2) * 2 + x // 2) * 4 + z) * 4 + y) * 2 + c


def move(value, x=0, y=0, z=0, c=0):
    pairs = []
    for px in range(4):
        for pz in range(4):
            for py in range(4):
                for pc in range(2):
                    target = ((px + x) % 4, (py + y) % 4, (pz + z) % 4, (pc + c) % 2)
                    pairs.append((device_index(px, py, pz, pc), device_index(*target)))
    return lax.ppermute(value, AXES, pairs)


def slide(value, lat, lon):
    pairs = []
    for row in range(2):
        for col in range(64):
            pairs.append((row * 64 + col, (row + lat) % 2 * 64 + (col + lon) % 64))
    return lax.ppermute(value, AXES, pairs)


def half_of(value, which):
    width = value.shape[-1] // 2
    return lax.dynamic_slice_in_dim(value, which * width, width, value.ndim - 1)


def join_cores(mine, other, core, axis):
    return jnp.where(
        core == 0,
        jnp.concatenate([mine, other], axis=axis),
        jnp.concatenate([other, mine], axis=axis),
    )


def gather(block, axes, count):
    copies = jnp.broadcast_to(block[None], (count,) + block.shape)
    return lax.all_to_all(copies, axes, 0, 0, tiled=True)


def scatter(blocks, axes):
    return jnp.sum(lax.all_to_all(blocks, axes, 0, 0, tiled=True).astype(F32), axis=0)


def own_rows(block, core):
    rows = block.shape[0] // 2
    mine = lax.dynamic_slice_in_dim(block, core * rows, rows, 0)
    other = move(lax.dynamic_slice_in_dim(block, (1 - core) * rows, rows, 0), c=1)
    return join_cores(mine, other, core, 1)


def inner(left, right):
    return lax.dot_general(left, right, (((0,), (0,)), ((), ())), preferred_element_type=F32)


def rims(field, lat):
    width = field.shape[-1]
    near = lax.dynamic_slice_in_dim(field, (1 - lat) * SHIFT, SHIFT, 0)
    out = [slide(near, 1, 0)]
    for step in (1, -1):
        cut = slice(COLS - SHIFT, COLS) if step == 1 else slice(0, SHIFT)
        out.append(slide(field[:, cut].reshape(-1, width), 0, step))
        out.append(slide(near[:, cut].reshape(-1, width), 1, step))
    return out


def dot(left, right):
    return jnp.dot(left, right, preferred_element_type=F32)


def dot_t(left, right):
    return lax.dot_general(left, right, (((1,), (1,)), ((), ())), preferred_element_type=F32)


def lay_out(wide, own, across, west, west_far, east, east_far, groups, skipped=0):
    sides = [
        (0, west[...].astype(F32), west_far[...].astype(F32)),
        (SHIFT + COLS, east[...].astype(F32), east_far[...].astype(F32)),
    ]
    for group in range(groups):
        lanes = slice(group * LANES, (group + 1) * LANES)
        rim_lanes = slice(skipped + group * LANES, skipped + (group + 1) * LANES)
        for row in range(ROWS + SHIFT):
            centre = own[row, :, lanes] if row < ROWS else across[row - ROWS, :, rim_lanes]
            wide[group, row, SHIFT : SHIFT + COLS, :] = centre.astype(F32)
            for start, close, far in sides:
                part, at = (close, row) if row < ROWS else (far, row - ROWS)
                wide[group, row, start : start + SHIFT, :] = part[SHIFT * at : SHIFT * (at + 1), rim_lanes]


def chunks(row_pairs):
    for win in range(WINS):
        for pair in range(row_pairs):
            for parity in range(4):
                row = 2 * pair + parity // 2
                yield win, pair, parity, row, pl.ds(WIN * win + parity % 2, 4, stride=2)


def give_back(out, wide):
    for group in range(4):
        lanes = slice(group * LANES, (group + 1) * LANES)
        for row in range(ROWS):
            out[row, :, lanes] = wide[group, row, SHIFT : SHIFT + COLS, :].astype(BF16)


def own_mask(per_window, shape):
    index = lax.broadcasted_iota(jnp.int32, shape, 0)
    win = index // per_window
    cell = (index % per_window) % (CELLS if per_window % CELLS == 0 else OWN)
    west = (win == 0) & (cell % 4 < 2)
    east = (win == WINS - 1) & (cell % 4 >= 2)
    return ((cell < OWN) & ~west & ~east).astype(F32)


def head_sums(values):
    row = lax.broadcasted_iota(jnp.int32, (D, D), 0) // 64
    col = lax.broadcasted_iota(jnp.int32, (D, D), 1) // 64
    same = (row == col).astype(BF16)
    high = values.astype(BF16)
    low = (values - high.astype(F32)).astype(BF16)
    return dot(high, same) + dot(low, same)


def normalize(values):
    centre = values - jnp.mean(values, axis=-1, keepdims=True)
    scale = lax.rsqrt(jnp.mean(centre * centre, axis=-1, keepdims=True) + EPS_NORM)
    return centre * scale, scale


def normalize_back(grad, normed, scale):
    mean = jnp.mean(grad, axis=-1, keepdims=True)
    slope = jnp.mean(grad * normed, axis=-1, keepdims=True)
    return scale * (grad - mean - normed * slope)


def lane_halves():
    lane = lax.broadcasted_iota(jnp.int32, (1, LANES), 1)
    return [(lane < 64).astype(BF16), (lane >= 64).astype(BF16)]


def fine_forward_kernel(
    spot, logit, own, across, west, west_far, east, east_far, table, w_qkv, w_out,
    skip, merged_norm, merged_spread, normed, spread, units, unit_scale, weights, attended,
    wide, embedded,
):
    lay_out(wide, own, across, west, west_far, east, east_far, 5)
    for win, pair, parity, row, cols in chunks(6):
        at = win * PATCHES + parity * CELLS + pair * 4
        for group in range(5):
            embedded[at : at + 4, group * LANES : (group + 1) * LANES] = wide[group, row, cols, :]

    @pl.loop(0, WINS)
    def _(win):
        rows = pl.ds(pl.multiple_of(win * PATCHES, 32), PATCHES)
        kind = embedded[rows, D : D + 1]
        first, second, third = table[0:1, :], table[1:2, :], table[2:3, :]
        added = jnp.where(kind == 0.0, first, jnp.where(kind == 1.0, second, third))
        values = embedded[rows, :D] + added
        embedded[rows, :D] = values
        unit, scale = normalize(values)
        normed[rows, :] = unit.astype(BF16)
        spread[rows, :] = scale

    block = TOKENS // 3
    for part in range(3):
        columns = slice(part * D, (part + 1) * D)
        for start in range(0, TOKENS, block):
            rows = slice(start, start + block)
            values = dot(normed[rows, :], w_qkv[:, columns])
            if part < 2:
                scale = lax.rsqrt(head_sums(values * values) + EPS_UNIT)
                unit_scale[rows, columns] = scale
                values = values * scale
            units[rows, columns] = values.astype(BF16)

    halves = lane_halves()
    outer = []
    for axis in range(2):
        index = lax.broadcasted_iota(jnp.int32, (PATCHES, PATCHES), axis)
        outer.append(((index % CELLS) // 8 == spot[0]).astype(jnp.int32))
    same = outer[0] == outer[1]

    @pl.loop(0, WINS)
    def _(win):
        rows = pl.ds(pl.multiple_of(win * PATCHES, 32), PATCHES)
        for duo in range(4):
            lanes = slice(duo * LANES, (duo + 1) * LANES)
            queries = units[rows, lanes]
            keys = units[rows, D + duo * LANES : D + (duo + 1) * LANES]
            values = units[rows, 2 * D + duo * LANES : 2 * D + (duo + 1) * LANES]
            total = jnp.zeros((PATCHES, LANES), F32)
            for side in range(2):
                head = 2 * duo + side
                scores = dot_t(queries, keys * halves[side]) * logit[head]
                exponent = jnp.where(same, jnp.exp(scores), 0.0)
                share = exponent * (1.0 / jnp.sum(exponent, axis=-1, keepdims=True))
                share = share.astype(BF16)
                weights[win * HEADS + head] = share
                total = total + dot(share, values * halves[side])
            attended[rows, lanes] = total.astype(BF16)

    for start in range(0, TOKENS, block):
        rows = slice(start, start + block)
        projected = dot(attended[rows, :], w_out[...]).astype(BF16).astype(F32)
        embedded[rows, :D] = (embedded[rows, :D] + projected).astype(BF16).astype(F32)
    for win in range(WINS):
        for parity in range(4):
            at = win * PATCHES + parity * CELLS
            skip[win * CELLS : (win + 1) * CELLS, parity * D : (parity + 1) * D] = embedded[
                at : at + CELLS, :D
            ]
    unit, scale = normalize(skip[...])
    merged_norm[...] = unit.astype(BF16)
    merged_spread[...] = scale


def cotangent_kernel(own, across, west, west_far, east, east_far, merged, rounded, wide):
    lay_out(wide, own, across, west, west_far, east, east_far, 4, D + LANES)
    for win, pair, parity, row, cols in chunks(6):
        at = win * CELLS + pair * 4
        for group in range(4):
            lane = parity * D + group * LANES
            merged[at : at + 4, lane : lane + LANES] = wide[group, row, cols, :]
    rounded[...] = merged[...].astype(BF16)


def coarse_kernel(
    norm, norm_other, cot, cot_other, parts, coarse, grad_pre, split, blocks, merge, sem
):
    copy = pltpu.make_async_copy(parts, merge, sem)
    copy.start()
    copy.wait()
    w_merge = merge[:, :32, :].reshape(2048, 512)
    for j in range(2):
        pair = merge[:, 32 + 16 * j : 48 + 16 * j, :].astype(F32)
        for k in range(2):
            quarter = pair[:, 8 * k : 8 * k + 8, :].reshape(512, 512)
            column = (2 * j + k) * 512
            split[:, column : column + 512] = quarter.astype(BF16)
    slope = 0.7978845608028654
    cubic = 0.044715
    keep = own_mask(CELLS, (ALL_CELLS, 1))
    own_grads, own_cots = [], []
    for i, (unit, cotangent) in enumerate(((norm, cot), (norm_other, cot_other))):
        value = dot(unit[...], w_merge)
        square = value * value
        bend = jnp.tanh(slope * (value + cubic * (square * value)))
        half_bend = 0.5 * (1.0 + bend)
        coarse[i] = (value * half_bend).astype(BF16)
        rise = half_bend + 0.5 * value * (1.0 - bend * bend) * slope * (1.0 + 3.0 * cubic * square)
        grad = dot_t(cotangent[...], split[...]) * rise
        grad_pre[i] = grad.astype(BF16)
        own_grads.append((grad * keep).astype(BF16))
        own_cots.append((coarse[i].astype(F32) * keep).astype(BF16))
    for x in range(4):
        chips = slice(x * 16, (x + 1) * 16)
        lanes = slice(x * 512, (x + 1) * 512)
        block = inner(norm[:, lanes], own_grads[0]) + inner(norm_other[:, lanes], own_grads[1])
        blocks[chips, :32, :] = block.astype(BF16).reshape(16, 32, 512)
    for j in range(2):
        quarters = []
        for k in range(2):
            lanes = slice((2 * j + k) * 512, (2 * j + k + 1) * 512)
            block = inner(own_cots[0], cot[:, lanes]) + inner(own_cots[1], cot_other[:, lanes])
            quarters.append(block.reshape(64, 8, 512))
        pair = jnp.concatenate(quarters, axis=1).astype(BF16)
        blocks[:, 32 + 16 * j : 48 + 16 * j, :] = pair


def partial_kernel(
    parts, coarse, grad_pre, split, grad_mine, grad_other, out_mine, out_other, merge, sem
):
    copy = pltpu.make_async_copy(parts.at[:, :32], merge, sem)
    copy.start()
    for i, out in enumerate((out_mine, out_other)):
        out[...] = dot(coarse[i], split[...]).astype(out.dtype)
    copy.wait()
    w_merge = merge[...].reshape(2048, 512)
    for i, out in enumerate((grad_mine, grad_other)):
        out[...] = dot_t(grad_pre[i], w_merge).astype(out.dtype)


def decode_kernel(skip, out_mine, received, decoded, sum_m, wide):
    sum_m[...] = skip[...] + out_mine[...] + received[...].astype(F32)
    for win, pair, parity, row, cols in chunks(4):
        at = win * CELLS + pair * 4
        for group in range(4):
            lane = parity * D + group * LANES
            wide[group, row, cols, :] = sum_m[at : at + 4, lane : lane + LANES]
    give_back(decoded, wide)


def fine_backward_kernel(
    spot, logit, grad_mine, received, cot, merged_norm, merged_spread,
    units, unit_scale, weights, normed, attended, w_out,
    grad_skip, grad_packed, grads_mine, grads_other,
    grad_tokens, grad_att, grad_units,
):
    grad = (grad_mine[...] + received[...].astype(F32)).astype(BF16).astype(F32)
    grad_skip[...] = cot[...] + normalize_back(grad, merged_norm[...].astype(F32), merged_spread[...])
    for win in range(WINS):
        for parity in range(4):
            at = win * PATCHES + parity * CELLS
            grad_tokens[at : at + CELLS, :] = grad_skip[
                win * CELLS : (win + 1) * CELLS, parity * D : (parity + 1) * D
            ]
    block = TOKENS // 3
    for start in range(0, TOKENS, block):
        rows = slice(start, start + block)
        grad_att[rows, :] = dot_t(grad_tokens[rows, :].astype(BF16), w_out[...]).astype(BF16)
    halves = lane_halves()

    @pl.loop(0, WINS)
    def _(win):
        rows = pl.ds(pl.multiple_of(win * PATCHES, 32), PATCHES)
        for duo in range(4):
            lanes = slice(duo * LANES, (duo + 1) * LANES)
            key_lanes = slice(D + duo * LANES, D + (duo + 1) * LANES)
            value_lanes = slice(2 * D + duo * LANES, 2 * D + (duo + 1) * LANES)
            queries, keys, values = units[rows, lanes], units[rows, key_lanes], units[rows, value_lanes]
            grad_out = grad_att[rows, lanes]
            grad_q = jnp.zeros((PATCHES, LANES), F32)
            grad_k = jnp.zeros((PATCHES, LANES), F32)
            grad_v = jnp.zeros((PATCHES, LANES), F32)
            for side in range(2):
                head = 2 * duo + side
                half = halves[side]
                share = weights[win * HEADS + head]
                wide_share = share.astype(F32)
                flow = dot_t(grad_out, values * half) * wide_share
                flow = flow - wide_share * jnp.sum(flow, axis=-1, keepdims=True)
                flow = (flow * logit[head]).astype(BF16)
                grad_q = grad_q + dot(flow, keys * half)
                grad_k = grad_k + inner(flow, queries * half)
                grad_v = grad_v + inner(share, grad_out * half)
            grad_units[rows, lanes] = grad_q
            grad_units[rows, key_lanes] = grad_k
            grad_packed[rows, value_lanes] = grad_v.astype(BF16)

    for part in range(2):
        columns = slice(part * D, (part + 1) * D)
        for start in range(0, TOKENS, block):
            rows = slice(start, start + block)
            unit = units[rows, columns].astype(F32)
            grad = grad_units[rows, columns]
            along = head_sums(unit * grad)
            grad_packed[rows, columns] = (
                unit_scale[rows, columns] * (grad - unit * along)
            ).astype(BF16)
    keep = own_mask(PATCHES, (TOKENS, 1))
    own_grad = (grad_tokens[...] * keep).astype(BF16)
    own_normed = (normed[...].astype(F32) * keep).astype(BF16)
    for part in range(4):
        if part < 3:
            result = inner(own_normed, grad_packed[:, part * D : (part + 1) * D]).astype(BF16)
        else:
            result = inner(attended[...], own_grad).astype(BF16)
        lanes = slice(part % 2 * D, (part % 2 + 1) * D)

        @pl.when(spot[1] == part // 2)
        def _():
            grads_mine[:, lanes] = result

        @pl.when(spot[1] != part // 2)
        def _():
            grads_other[:, lanes] = result


def field_grad_kernel(grad_skip, grad_packed, normed, spread, w_qkv, grad_fields, total, wide):
    block = TOKENS // 3
    for start in range(0, TOKENS, block):
        rows = slice(start, start + block)
        grad = dot_t(grad_packed[rows, :], w_qkv[...]).astype(BF16).astype(F32)
        total[rows, :] = normalize_back(grad, normed[rows, :].astype(F32), spread[rows, :])
    for win, pair, parity, row, cols in chunks(4):
        at = win * PATCHES + parity * CELLS + pair * 4
        cell = win * CELLS + pair * 4
        for group in range(4):
            lanes = slice(group * LANES, (group + 1) * LANES)
            lane = parity * D + group * LANES
            wide[group, row, cols, :] = (
                total[at : at + 4, lanes] + grad_skip[cell : cell + 4, lane : lane + LANES]
            )
    give_back(grad_fields, wide)


def kernel_call(
    kernel, name, outs, scratch, args, scalars=0, ahead=0, in_place=0, flops=0, moved=0, curves=0
):
    count = len(args)
    specs = []
    for index in range(count):
        if index < scalars:
            specs.append(pl.BlockSpec(memory_space=pltpu.SMEM))
        elif index < ahead or index >= count - in_place:
            specs.append(pl.BlockSpec(memory_space=pl.ANY))
        else:
            specs.append(pl.BlockSpec(memory_space=pltpu.VMEM))
    shapes = [jax.ShapeDtypeStruct(shape, dtype) for shape, dtype in outs]
    return pl.pallas_call(
        kernel,
        out_shape=shapes,
        in_specs=specs,
        out_specs=[pl.BlockSpec(memory_space=pltpu.VMEM)] * len(outs),
        scratch_shapes=scratch,
        compiler_params=pltpu.CompilerParams(vmem_limit_bytes=VMEM_BYTES),
        cost_estimate=pl.CostEstimate(flops=flops, bytes_accessed=moved, transcendentals=curves),
        name=name,
    )(*args)


def per_device(
    fields, surface, surface_table, logit_scale, w_qkv, w_out, w_merge, w_split, cotangent
):
    core = lax.axis_index("c")
    lat = lax.axis_index("xl")
    spot = jnp.stack([lat, core]).astype(jnp.int32)
    kinds = jnp.broadcast_to(surface.astype(BF16)[:, :, None], (ROWS, COLS, LANES))
    own_fields = jnp.concatenate([fields, kinds], axis=-1)
    rim = rims(jnp.concatenate([own_fields, cotangent], axis=-1), lat)

    index = jnp.arange(1024, dtype=jnp.int32)
    source = index % 512 // 8 * 16 + index // 512 * 8 + index % 8
    runs = (index[:, None] == source[None, :]).astype(BF16)
    sorted_merge = jnp.dot(w_merge, runs, preferred_element_type=F32).astype(BF16)
    far = move(half_of(sorted_merge, 1 - core), c=1)
    merge_block = join_cores(half_of(sorted_merge, core), far, core, 0)
    split_block = w_split.reshape(8, 4, 512).transpose(1, 0, 2).reshape(32, 512)
    block = jnp.concatenate([merge_block, split_block], axis=0)
    *rim, block = lax.optimization_barrier((*rim, block))
    mine = gather(block, CHIP_AXES, 64)

    cells = (ALL_CELLS, 4 * D)
    skip, merged_norm, merged_spread, normed, spread, units, unit_scale, weights, attended = kernel_call(
        fine_forward_kernel,
        "fine_forward",
        [
            (cells, F32),
            (cells, BF16),
            ((ALL_CELLS, 1), F32),
            ((TOKENS, D), BF16),
            ((TOKENS, 1), F32),
            ((TOKENS, 3 * D), BF16),
            ((TOKENS, 2 * D), F32),
            ((WINS * HEADS, PATCHES, PATCHES), BF16),
            ((TOKENS, D), BF16),
        ],
        [pltpu.VMEM((5, 12, 72, LANES), F32), pltpu.VMEM((TOKENS, D + LANES), F32)],
        (spot, logit_scale, own_fields, *rim, surface_table, w_qkv, w_out),
        scalars=2,
        flops=15_000_000_000,
        moved=12_000_000,
    )
    cot, cot_rounded = kernel_call(
        cotangent_kernel,
        "cotangent_cells",
        [(cells, F32), (cells, BF16)],
        [pltpu.VMEM((4, 12, 72, LANES), F32)],
        (cotangent, *rim),
        moved=8_000_000,
    )
    norm_other, cot_other = move(merged_norm, c=1), move(cot_rounded, c=1)
    norm_other, cot_other, mine = lax.optimization_barrier((norm_other, cot_other, mine))
    coarse, grad_pre, split, blocks = kernel_call(
        coarse_kernel,
        "coarse",
        [
            ((2, ALL_CELLS, 512), BF16),
            ((2, ALL_CELLS, 512), BF16),
            ((512, 2048), BF16),
            ((64, 64, 512), BF16),
        ],
        [pltpu.VMEM((64, 64, 512), BF16), pltpu.SemaphoreType.DMA],
        (merged_norm, norm_other, cot_rounded, cot_other, mine),
        in_place=1,
        flops=8_000_000_000,
        moved=15_000_000,
    )
    split, blocks = lax.optimization_barrier((split, blocks))
    blocks = scatter(blocks, CHIP_AXES)
    grad_mine, grad_other, out_mine, out_other = kernel_call(
        partial_kernel,
        "partial_products",
        [(cells, F32), (cells, BF16), (cells, F32), (cells, BF16)],
        [pltpu.VMEM((64, 32, 512), BF16), pltpu.SemaphoreType.DMA],
        (mine, coarse, grad_pre, split),
        ahead=1,
        flops=3_000_000_000,
        moved=10_000_000,
    )
    grad_skip, grad_packed, fine_mine, fine_other = kernel_call(
        fine_backward_kernel,
        "fine_backward",
        [(cells, F32), ((TOKENS, 3 * D), BF16), ((D, 1024), BF16), ((D, 1024), BF16)],
        [
            pltpu.VMEM((TOKENS, D), F32),
            pltpu.VMEM((TOKENS, D), BF16),
            pltpu.VMEM((TOKENS, 2 * D), F32),
        ],
        (
            spot,
            logit_scale,
            grad_mine,
            move(grad_other, c=1),
            cot,
            merged_norm,
            merged_spread,
            units,
            unit_scale,
            weights,
            normed,
            attended,
            w_out,
        ),
        scalars=2,
        flops=15_000_000_000,
        moved=15_000_000,
    )
    (decoded,) = kernel_call(
        decode_kernel,
        "decode",
        [((ROWS, COLS, D), BF16)],
        [pltpu.VMEM(cells, F32), pltpu.VMEM((4, 8, 72, LANES), F32)],
        (skip, out_mine, move(out_other, c=1)),
        moved=8_000_000,
    )
    (grad_fields,) = kernel_call(
        field_grad_kernel,
        "field_grad",
        [((ROWS, COLS, D), BF16)],
        [pltpu.VMEM((TOKENS, D), F32), pltpu.VMEM((4, 8, 72, LANES), F32)],
        (grad_skip, grad_packed, normed, spread, w_qkv),
        flops=4_000_000_000,
        moved=8_000_000,
    )
    fine_half = (fine_mine.astype(F32) + move(fine_other, c=1).astype(F32)).astype(BF16)
    fine_half, blocks = lax.optimization_barrier((fine_half, blocks))
    fine_grads = own_rows(scatter(fine_half.reshape(64, D // 64, 1024), CHIP_AXES), core)
    grad_split = blocks[32:].reshape(4, 8, 512).transpose(1, 0, 2).reshape(8, 2048)
    grad_merge = own_rows(blocks[:32], core).reshape(16, 2, 64, 8).transpose(0, 2, 1, 3)
    return (
        decoded,
        grad_fields,
        fine_grads[:, : 3 * D],
        fine_grads[:, 3 * D :],
        grad_merge.reshape(16, 1024),
        grad_split,
    )


def solution(mesh):
    fine_mesh = Mesh(mesh.devices.reshape(2, 2, 4, 4, 2), AXES)
    grid, rows = P("xl", LON, None), P(AXES, None)
    in_specs = (grid, P("xl", LON), P(), P(), P(), P(), rows, rows, grid)
    out_specs = (grid, grid, rows, rows, rows, rows)
    return jax.shard_map(
        per_device, mesh=fine_mesh, in_specs=in_specs, out_specs=out_specs, check_vma=False
    )
```

```python
import functools

import jax
import jax.numpy as jnp
from jax import lax
from jax.experimental import pallas as pl
from jax.experimental.pallas import tpu as pltpu
from jax.sharding import Mesh, PartitionSpec as P

HEADS = 8
WIN = 8
SHIFT = 4
EPS_NORM = 1e-05
EPS_UNIT = 1e-06

D = 512
ROWS, COLS = 8, 64
WINS = COLS // WIN + 1
CELLS = 24
OWN = 16
PATCHES = 4 * CELLS
TOKENS = WINS * PATCHES
ALL_CELLS = WINS * CELLS
OWN_CELLS = WINS * OWN
LANES = 128
VMEM_BYTES = 48 * 1024 * 1024

AXES = ("xl", "xh", "z", "y", "c")
CHIP_AXES = ("xl", "xh", "z", "y")
LON = ("xh", "z", "y", "c")

F32 = jnp.float32
BF16 = jnp.bfloat16


def device_index(x, y, z, c):
    return ((((x % 2) * 2 + x // 2) * 4 + z) * 4 + y) * 2 + c


def move(value, x=0, y=0, z=0, c=0):
    pairs = []
    for px in range(4):
        for pz in range(4):
            for py in range(4):
                for pc in range(2):
                    target = ((px + x) % 4, (py + y) % 4, (pz + z) % 4, (pc + c) % 2)
                    pairs.append((device_index(px, py, pz, pc), device_index(*target)))
    return lax.ppermute(value, AXES, pairs)


def slide(value, lat, lon):
    pairs = []
    for row in range(2):
        for col in range(64):
            pairs.append((row * 64 + col, (row + lat) % 2 * 64 + (col + lon) % 64))
    return lax.ppermute(value, AXES, pairs)


def half_of(value, which):
    width = value.shape[-1] // 2
    return lax.dynamic_slice_in_dim(value, which * width, width, value.ndim - 1)


def join_cores(mine, other, core, axis):
    return jnp.where(
        core == 0,
        jnp.concatenate([mine, other], axis=axis),
        jnp.concatenate([other, mine], axis=axis),
    )


def add_blocks(blocks):
    return jnp.sum(blocks.astype(F32), axis=0)


def own_rows(block, core):
    rows = block.shape[0] // 2
    mine = lax.dynamic_slice_in_dim(block, core * rows, rows, 0)
    other = move(lax.dynamic_slice_in_dim(block, (1 - core) * rows, rows, 0), c=1)
    return join_cores(mine, other, core, 1)


def inner(left, right):
    return lax.dot_general(left, right, (((0,), (0,)), ((), ())), preferred_element_type=F32)


def rims(fields, lat, before):
    def cut(start, cols):
        part = [field[:, start : start + cols] for field in fields]
        close = [field.reshape(-1, field.shape[-1]) for field in part]
        far = [lax.dynamic_slice_in_dim(field, (1 - lat) * SHIFT, SHIFT, 0) for field in part]
        far = [field.reshape(-1, field.shape[-1]) for field in far]
        return jnp.concatenate(close, axis=-1), jnp.concatenate(far, axis=-1)

    near = [lax.dynamic_slice_in_dim(field, (1 - lat) * SHIFT, SHIFT, 0) for field in fields]
    across = slide(jnp.concatenate(near, axis=-1), 1, 0)
    *fields, before = lax.optimization_barrier((*fields, before))
    out = [across]
    for step in (1, -1):
        close, far = cut(COLS - SHIFT if step == 1 else 0, SHIFT)
        out.append(slide(close, 0, step))
        out.append(slide(far, 1, step))
    return out, before


def dot(left, right):
    return jnp.dot(left, right, preferred_element_type=F32)


def dot_t(left, right):
    return lax.dot_general(left, right, (((1,), (1,)), ((), ())), preferred_element_type=F32)


def lay_out(wide, own, across, west, west_far, east, east_far, groups, skipped=0):
    sides = [
        (0, west[...].astype(F32), west_far[...].astype(F32)),
        (SHIFT + COLS, east[...].astype(F32), east_far[...].astype(F32)),
    ]
    for group in range(groups):
        lanes = slice(group * LANES, (group + 1) * LANES)
        rim_lanes = slice(skipped + group * LANES, skipped + (group + 1) * LANES)
        for row in range(ROWS + SHIFT):
            centre = own[row, :, lanes] if row < ROWS else across[row - ROWS, :, rim_lanes]
            wide[group, row, SHIFT : SHIFT + COLS, :] = centre.astype(F32)
            for start, close, far in sides:
                part, at = (close, row) if row < ROWS else (far, row - ROWS)
                wide[group, row, start : start + SHIFT, :] = part[SHIFT * at : SHIFT * (at + 1), rim_lanes]


def chunks(row_pairs):
    for win in range(WINS):
        for pair in range(row_pairs):
            for parity in range(4):
                row = 2 * pair + parity // 2
                yield win, pair, parity, row, pl.ds(WIN * win + parity % 2, 4, stride=2)


def give_back(out, wide):
    for group in range(4):
        lanes = slice(group * LANES, (group + 1) * LANES)
        for row in range(ROWS):
            out[row, :, lanes] = wide[group, row, SHIFT : SHIFT + COLS, :].astype(BF16)


def own_mask(per_window, shape):
    index = lax.broadcasted_iota(jnp.int32, shape, 0)
    win = index // per_window
    cell = (index % per_window) % (CELLS if per_window % CELLS == 0 else OWN)
    west = (win == 0) & (cell % 4 < 2)
    east = (win == WINS - 1) & (cell % 4 >= 2)
    return ((cell < OWN) & ~west & ~east).astype(F32)


def head_sums(values):
    row = lax.broadcasted_iota(jnp.int32, (D, D), 0) // 64
    col = lax.broadcasted_iota(jnp.int32, (D, D), 1) // 64
    same = (row == col).astype(BF16)
    high = values.astype(BF16)
    low = (values - high.astype(F32)).astype(BF16)
    return dot(high, same) + dot(low, same)


def normalize(values):
    centre = values - jnp.mean(values, axis=-1, keepdims=True)
    scale = lax.rsqrt(jnp.mean(centre * centre, axis=-1, keepdims=True) + EPS_NORM)
    return centre * scale, scale


def normalize_back(grad, normed, scale):
    mean = jnp.mean(grad, axis=-1, keepdims=True)
    slope = jnp.mean(grad * normed, axis=-1, keepdims=True)
    return scale * (grad - mean - normed * slope)


def lane_halves():
    lane = lax.broadcasted_iota(jnp.int32, (1, LANES), 1)
    return [(lane < 64).astype(BF16), (lane >= 64).astype(BF16)]


def fine_forward_kernel(
    spot, logit, own, across, west, west_far, east, east_far, table, w_qkv, w_out,
    skip, merged_norm, merged_spread, normed, spread, units, unit_scale, weights, attended,
    wide, embedded,
):
    lay_out(wide, own, across, west, west_far, east, east_far, 5)
    for win, pair, parity, row, cols in chunks(6):
        at = win * PATCHES + parity * CELLS + pair * 4
        for group in range(5):
            embedded[at : at + 4, group * LANES : (group + 1) * LANES] = wide[group, row, cols, :]

    @pl.loop(0, WINS)
    def _(win):
        rows = pl.ds(pl.multiple_of(win * PATCHES, 32), PATCHES)
        kind = embedded[rows, D : D + 1]
        first, second, third = table[0:1, :], table[1:2, :], table[2:3, :]
        added = jnp.where(kind == 0.0, first, jnp.where(kind == 1.0, second, third))
        values = embedded[rows, :D] + added
        embedded[rows, :D] = values
        unit, scale = normalize(values)
        normed[rows, :] = unit.astype(BF16)
        spread[rows, :] = scale

    block = TOKENS // 3
    for part in range(3):
        columns = slice(part * D, (part + 1) * D)
        for start in range(0, TOKENS, block):
            rows = slice(start, start + block)
            values = dot(normed[rows, :], w_qkv[:, columns])
            if part < 2:
                scale = lax.rsqrt(head_sums(values * values) + EPS_UNIT)
                unit_scale[rows, columns] = scale
                values = values * scale
            units[rows, columns] = values.astype(BF16)

    halves = lane_halves()
    outer = []
    for axis in range(2):
        index = lax.broadcasted_iota(jnp.int32, (PATCHES, PATCHES), axis)
        outer.append(((index % CELLS) // 8 == spot[0]).astype(jnp.int32))
    same = outer[0] == outer[1]

    @pl.loop(0, WINS)
    def _(win):
        rows = pl.ds(pl.multiple_of(win * PATCHES, 32), PATCHES)
        for duo in range(4):
            lanes = slice(duo * LANES, (duo + 1) * LANES)
            queries = units[rows, lanes]
            keys = units[rows, D + duo * LANES : D + (duo + 1) * LANES]
            values = units[rows, 2 * D + duo * LANES : 2 * D + (duo + 1) * LANES]
            total = jnp.zeros((PATCHES, LANES), F32)
            for side in range(2):
                head = 2 * duo + side
                scores = dot_t(queries, keys * halves[side]) * logit[head]
                exponent = jnp.where(same, jnp.exp(scores), 0.0)
                share = exponent * (1.0 / jnp.sum(exponent, axis=-1, keepdims=True))
                share = share.astype(BF16)
                weights[win * HEADS + head] = share
                total = total + dot(share, values * halves[side])
            attended[rows, lanes] = total.astype(BF16)

    for start in range(0, TOKENS, block):
        rows = slice(start, start + block)
        projected = dot(attended[rows, :], w_out[...]).astype(BF16).astype(F32)
        embedded[rows, :D] = (embedded[rows, :D] + projected).astype(BF16).astype(F32)
    for win in range(WINS):
        for parity in range(4):
            at = win * PATCHES + parity * CELLS
            skip[win * CELLS : (win + 1) * CELLS, parity * D : (parity + 1) * D] = embedded[
                at : at + CELLS, :D
            ]
    unit, scale = normalize(skip[...])
    merged_norm[...] = unit.astype(BF16)
    merged_spread[...] = scale


def spread_kernel(block, copies):
    for chip in range(64):
        copies[chip] = block[...]


def cotangent_kernel(own, across, west, west_far, east, east_far, merged, rounded, wide):
    lay_out(wide, own, across, west, west_far, east, east_far, 4, D + LANES)
    for win, pair, parity, row, cols in chunks(6):
        at = win * CELLS + pair * 4
        for group in range(4):
            lane = parity * D + group * LANES
            merged[at : at + 4, lane : lane + LANES] = wide[group, row, cols, :]
    rounded[...] = merged[...].astype(BF16)


def coarse_kernel(
    norm, norm_other, cot, cot_other, parts,
    coarse_out, grad_out, split, blocks,
    merge, packed, coarse, grad_pre, sems,
):
    load_merge = pltpu.make_async_copy(parts.at[:, :32], merge, sems.at[0])
    load_split = pltpu.make_async_copy(parts.at[:, 32:], packed, sems.at[1])
    store_coarse = pltpu.make_async_copy(coarse, coarse_out, sems.at[2])
    store_grad = pltpu.make_async_copy(grad_pre, grad_out, sems.at[3])
    load_split.start()
    load_merge.start()
    load_split.wait()
    for j in range(2):
        pair = packed[:, 16 * j : 16 * j + 16, :].astype(F32)
        for k in range(2):
            quarter = pair[:, 8 * k : 8 * k + 8, :].reshape(512, 512)
            column = (2 * j + k) * 512
            split[:, column : column + 512] = quarter.astype(BF16)
    load_merge.wait()
    w_merge = merge[...].reshape(2048, 512)
    slope = 0.7978845608028654
    cubic = 0.044715
    keep = own_mask(CELLS, (ALL_CELLS, 1))
    own_grads, own_cots = [], []
    for i, (unit, cotangent) in enumerate(((norm, cot), (norm_other, cot_other))):
        value = dot(unit[...], w_merge)
        square = value * value
        bend = jnp.tanh(slope * (value + cubic * (square * value)))
        half_bend = 0.5 * (1.0 + bend)
        coarse[i] = (value * half_bend).astype(BF16)
        rise = half_bend + 0.5 * value * (1.0 - bend * bend) * slope * (1.0 + 3.0 * cubic * square)
        grad = dot_t(cotangent[...], split[...]) * rise
        grad_pre[i] = grad.astype(BF16)
        own_grads.append((grad * keep).astype(BF16))
        own_cots.append((coarse[i].astype(F32) * keep).astype(BF16))
    store_coarse.start()
    store_grad.start()
    for x in range(4):
        chips = slice(x * 16, (x + 1) * 16)
        lanes = slice(x * 512, (x + 1) * 512)
        block = inner(norm[:, lanes], own_grads[0]) + inner(norm_other[:, lanes], own_grads[1])
        blocks[chips, :32, :] = block.astype(BF16).reshape(16, 32, 512)
    for j in range(2):
        quarters = []
        for k in range(2):
            lanes = slice((2 * j + k) * 512, (2 * j + k + 1) * 512)
            block = inner(own_cots[0], cot[:, lanes]) + inner(own_cots[1], cot_other[:, lanes])
            quarters.append(block.reshape(64, 8, 512))
        pair = jnp.concatenate(quarters, axis=1).astype(BF16)
        blocks[:, 32 + 16 * j : 48 + 16 * j, :] = pair
    store_coarse.wait()
    store_grad.wait()


def partial_kernel(
    parts, coarse, grad_pre, split, grad_mine, grad_other, out_mine, out_other, merge, sem
):
    copy = pltpu.make_async_copy(parts.at[:, :32], merge, sem)
    copy.start()
    for i, out in enumerate((out_mine, out_other)):
        out[...] = dot(coarse[i], split[...]).astype(out.dtype)
    copy.wait()
    w_merge = merge[...].reshape(2048, 512)
    for i, out in enumerate((grad_mine, grad_other)):
        out[...] = dot_t(grad_pre[i], w_merge).astype(out.dtype)


def decode_kernel(skip, out_mine, received, decoded, sum_m, wide):
    sum_m[...] = skip[...] + out_mine[...] + received[...].astype(F32)
    for win, pair, parity, row, cols in chunks(4):
        at = win * CELLS + pair * 4
        for group in range(4):
            lane = parity * D + group * LANES
            wide[group, row, cols, :] = sum_m[at : at + 4, lane : lane + LANES]
    give_back(decoded, wide)


def fine_backward_kernel(
    spot, logit, grad_mine, received, cot, merged_norm, merged_spread,
    units, unit_scale, weights, normed, attended, w_out,
    grad_skip, grad_packed, grads_mine, grads_other,
    grad_tokens, grad_att, grad_units,
):
    grad = (grad_mine[...] + received[...].astype(F32)).astype(BF16).astype(F32)
    grad_skip[...] = cot[...] + normalize_back(grad, merged_norm[...].astype(F32), merged_spread[...])
    for win in range(WINS):
        for parity in range(4):
            at = win * PATCHES + parity * CELLS
            grad_tokens[at : at + CELLS, :] = grad_skip[
                win * CELLS : (win + 1) * CELLS, parity * D : (parity + 1) * D
            ]
    block = TOKENS // 3
    for start in range(0, TOKENS, block):
        rows = slice(start, start + block)
        grad_att[rows, :] = dot_t(grad_tokens[rows, :].astype(BF16), w_out[...]).astype(BF16)
    halves = lane_halves()

    @pl.loop(0, WINS)
    def _(win):
        rows = pl.ds(pl.multiple_of(win * PATCHES, 32), PATCHES)
        for duo in range(4):
            lanes = slice(duo * LANES, (duo + 1) * LANES)
            key_lanes = slice(D + duo * LANES, D + (duo + 1) * LANES)
            value_lanes = slice(2 * D + duo * LANES, 2 * D + (duo + 1) * LANES)
            queries, keys, values = units[rows, lanes], units[rows, key_lanes], units[rows, value_lanes]
            grad_out = grad_att[rows, lanes]
            grad_q = jnp.zeros((PATCHES, LANES), F32)
            grad_k = jnp.zeros((PATCHES, LANES), F32)
            grad_v = jnp.zeros((PATCHES, LANES), F32)
            for side in range(2):
                head = 2 * duo + side
                half = halves[side]
                share = weights[win * HEADS + head]
                wide_share = share.astype(F32)
                flow = dot_t(grad_out, values * half) * wide_share
                flow = flow - wide_share * jnp.sum(flow, axis=-1, keepdims=True)
                flow = (flow * logit[head]).astype(BF16)
                grad_q = grad_q + dot(flow, keys * half)
                grad_k = grad_k + inner(flow, queries * half)
                grad_v = grad_v + inner(share, grad_out * half)
            grad_units[rows, lanes] = grad_q
            grad_units[rows, key_lanes] = grad_k
            grad_packed[rows, value_lanes] = grad_v.astype(BF16)

    for part in range(2):
        columns = slice(part * D, (part + 1) * D)
        for start in range(0, TOKENS, block):
            rows = slice(start, start + block)
            unit = units[rows, columns].astype(F32)
            grad = grad_units[rows, columns]
            along = head_sums(unit * grad)
            grad_packed[rows, columns] = (
                unit_scale[rows, columns] * (grad - unit * along)
            ).astype(BF16)
    keep = own_mask(PATCHES, (TOKENS, 1))
    own_grad = (grad_tokens[...] * keep).astype(BF16)
    own_normed = (normed[...].astype(F32) * keep).astype(BF16)
    for part in range(4):
        if part < 3:
            result = inner(own_normed, grad_packed[:, part * D : (part + 1) * D]).astype(BF16)
        else:
            result = inner(attended[...], own_grad).astype(BF16)
        lanes = slice(part % 2 * D, (part % 2 + 1) * D)

        @pl.when(spot[1] == part // 2)
        def _():
            grads_mine[:, lanes] = result

        @pl.when(spot[1] != part // 2)
        def _():
            grads_other[:, lanes] = result


def field_grad_kernel(grad_skip, grad_packed, normed, spread, w_qkv, grad_fields, total, wide):
    block = TOKENS // 3
    for start in range(0, TOKENS, block):
        rows = slice(start, start + block)
        grad = dot_t(grad_packed[rows, :], w_qkv[...]).astype(BF16).astype(F32)
        total[rows, :] = normalize_back(grad, normed[rows, :].astype(F32), spread[rows, :])
    for win, pair, parity, row, cols in chunks(4):
        at = win * PATCHES + parity * CELLS + pair * 4
        cell = win * CELLS + pair * 4
        for group in range(4):
            lanes = slice(group * LANES, (group + 1) * LANES)
            lane = parity * D + group * LANES
            wide[group, row, cols, :] = (
                total[at : at + 4, lanes] + grad_skip[cell : cell + 4, lane : lane + LANES]
            )
    give_back(grad_fields, wide)


def kernel_call(
    kernel, name, outs, scratch, args, scalars=0, ahead=0, in_place=0, far_outs=0, flops=0, moved=0
):
    count = len(args)
    specs = []
    for index in range(count):
        if index < scalars:
            specs.append(pl.BlockSpec(memory_space=pltpu.SMEM))
        elif index < ahead or index >= count - in_place:
            specs.append(pl.BlockSpec(memory_space=pl.ANY))
        else:
            specs.append(pl.BlockSpec(memory_space=pltpu.VMEM))
    shapes = [jax.ShapeDtypeStruct(shape, dtype) for shape, dtype in outs]
    return pl.pallas_call(
        kernel,
        out_shape=shapes,
        in_specs=specs,
        out_specs=[
            pl.BlockSpec(memory_space=pl.ANY if index < far_outs else pltpu.VMEM)
            for index in range(len(outs))
        ],
        scratch_shapes=scratch,
        compiler_params=pltpu.CompilerParams(vmem_limit_bytes=VMEM_BYTES),
        cost_estimate=pl.CostEstimate(flops=flops, bytes_accessed=moved, transcendentals=0),
        name=name,
    )(*args)


def per_device(
    fields, surface, surface_table, logit_scale, w_qkv, w_out, w_merge, w_split, cotangent
):
    core = lax.axis_index("c")
    lat = lax.axis_index("xl")
    spot = jnp.stack([lat, core]).astype(jnp.int32)
    kinds = jnp.broadcast_to(surface.astype(BF16)[:, :, None], (ROWS, COLS, LANES))
    own_fields = jnp.concatenate([fields, kinds], axis=-1)

    index = jnp.arange(1024, dtype=jnp.int32)
    source = index % 512 // 8 * 16 + index // 512 * 8 + index % 8
    runs = (index[:, None] == source[None, :]).astype(BF16)
    sorted_merge = jnp.dot(w_merge, runs, preferred_element_type=F32).astype(BF16)
    far = move(half_of(sorted_merge, 1 - core), c=1)
    rim, far = rims((fields, kinds, cotangent), lat, far)
    merge_block = join_cores(half_of(sorted_merge, core), far, core, 0)
    split_block = w_split.reshape(8, 4, 512).transpose(1, 0, 2).reshape(32, 512)
    block = jnp.concatenate([merge_block, split_block], axis=0)
    (copies,) = kernel_call(
        spread_kernel, "spread_weights", [((64, 64, 512), BF16)], [], (block,), moved=4_000_000
    )
    *rim, copies = lax.optimization_barrier((*rim, copies))
    mine = lax.all_to_all(copies, CHIP_AXES, 0, 0, tiled=True)

    cells = (ALL_CELLS, 4 * D)
    skip, merged_norm, merged_spread, normed, spread, units, unit_scale, weights, attended = kernel_call(
        fine_forward_kernel,
        "fine_forward",
        [
            (cells, F32),
            (cells, BF16),
            ((ALL_CELLS, 1), F32),
            ((TOKENS, D), BF16),
            ((TOKENS, 1), F32),
            ((TOKENS, 3 * D), BF16),
            ((TOKENS, 2 * D), F32),
            ((WINS * HEADS, PATCHES, PATCHES), BF16),
            ((TOKENS, D), BF16),
        ],
        [pltpu.VMEM((5, 12, 72, LANES), F32), pltpu.VMEM((TOKENS, D + LANES), F32)],
        (spot, logit_scale, own_fields, *rim, surface_table, w_qkv, w_out),
        scalars=2,
        flops=15_000_000_000,
        moved=12_000_000,
    )
    cot, cot_rounded = kernel_call(
        cotangent_kernel,
        "cotangent_cells",
        [(cells, F32), (cells, BF16)],
        [pltpu.VMEM((4, 12, 72, LANES), F32)],
        (cotangent, *rim),
        moved=8_000_000,
    )
    norm_other, cot_other = move(merged_norm, c=1), move(cot_rounded, c=1)
    merged_spread, mine = lax.optimization_barrier((merged_spread, mine))
    coarse, grad_pre, split, blocks = kernel_call(
        coarse_kernel,
        "coarse",
        [
            ((2, ALL_CELLS, 512), BF16),
            ((2, ALL_CELLS, 512), BF16),
            ((512, 2048), BF16),
            ((64, 64, 512), BF16),
        ],
        [
            pltpu.VMEM((64, 32, 512), BF16),
            pltpu.VMEM((64, 32, 512), BF16),
            pltpu.VMEM((2, ALL_CELLS, 512), BF16),
            pltpu.VMEM((2, ALL_CELLS, 512), BF16),
            pltpu.SemaphoreType.DMA((4,)),
        ],
        (merged_norm, norm_other, cot_rounded, cot_other, mine),
        in_place=1,
        far_outs=2,
        flops=8_000_000_000,
        moved=15_000_000,
    )
    split, blocks = lax.optimization_barrier((split, blocks))
    blocks = lax.all_to_all(blocks, CHIP_AXES, 0, 0, tiled=True)
    grad_mine, grad_other, out_mine, out_other = kernel_call(
        partial_kernel,
        "partial_products",
        [(cells, F32), (cells, BF16), (cells, F32), (cells, BF16)],
        [pltpu.VMEM((64, 32, 512), BF16), pltpu.SemaphoreType.DMA],
        (mine, coarse, grad_pre, split),
        ahead=1,
        flops=3_000_000_000,
        moved=10_000_000,
    )
    grad_skip, grad_packed, fine_mine, fine_other = kernel_call(
        fine_backward_kernel,
        "fine_backward",
        [(cells, F32), ((TOKENS, 3 * D), BF16), ((D, 1024), BF16), ((D, 1024), BF16)],
        [
            pltpu.VMEM((TOKENS, D), F32),
            pltpu.VMEM((TOKENS, D), BF16),
            pltpu.VMEM((TOKENS, 2 * D), F32),
        ],
        (
            spot,
            logit_scale,
            grad_mine,
            move(grad_other, c=1),
            cot,
            merged_norm,
            merged_spread,
            units,
            unit_scale,
            weights,
            normed,
            attended,
            w_out,
        ),
        scalars=2,
        flops=15_000_000_000,
        moved=15_000_000,
    )
    (decoded,) = kernel_call(
        decode_kernel,
        "decode",
        [((ROWS, COLS, D), BF16)],
        [pltpu.VMEM(cells, F32), pltpu.VMEM((4, 8, 72, LANES), F32)],
        (skip, out_mine, move(out_other, c=1)),
        moved=8_000_000,
    )
    (grad_fields,) = kernel_call(
        field_grad_kernel,
        "field_grad",
        [((ROWS, COLS, D), BF16)],
        [pltpu.VMEM((TOKENS, D), F32), pltpu.VMEM((4, 8, 72, LANES), F32)],
        (grad_skip, grad_packed, normed, spread, w_qkv),
        flops=4_000_000_000,
        moved=8_000_000,
    )
    fine_half = (fine_mine.astype(F32) + move(fine_other, c=1).astype(F32)).astype(BF16)
    fine_half, blocks = lax.optimization_barrier((fine_half, blocks))
    fine_blocks = lax.all_to_all(fine_half.reshape(64, D // 64, 1024), CHIP_AXES, 0, 0, tiled=True)
    fine_sum = add_blocks(fine_blocks)
    fine_own = lax.dynamic_slice_in_dim(fine_sum, core * 4, 4, 0)
    fine_far = move(lax.dynamic_slice_in_dim(fine_sum, (1 - core) * 4, 4, 0), c=1)
    first, second = jnp.where(core == 0, fine_own, fine_far), jnp.where(core == 0, fine_far, fine_own)
    blocks = add_blocks(blocks)
    grad_split = blocks[32:].reshape(4, 8, 512).transpose(1, 0, 2).reshape(8, 2048)
    grad_merge = own_rows(blocks[:32], core).reshape(16, 2, 64, 8).transpose(0, 2, 1, 3)
    return (
        decoded,
        grad_fields,
        jnp.concatenate([first, second[:, :D]], axis=1),
        second[:, D:],
        grad_merge.reshape(16, 1024),
        grad_split,
    )


def solution(mesh):
    fine_mesh = Mesh(mesh.devices.reshape(2, 2, 4, 4, 2), AXES)
    grid, rows = P("xl", LON, None), P(AXES, None)
    in_specs = (grid, P("xl", LON), P(), P(), P(), P(), rows, rows, grid)
    out_specs = (grid, grid, rows, rows, rows, rows)
    return jax.shard_map(
        per_device, mesh=fine_mesh, in_specs=in_specs, out_specs=out_specs, check_vma=False
    )
```

```python
import functools

import jax
import jax.numpy as jnp
from jax import lax
from jax.experimental import pallas as pl
from jax.experimental.pallas import tpu as pltpu
from jax.sharding import Mesh, PartitionSpec as P

HEADS = 8
WIN = 8
SHIFT = 4
EPS_NORM = 1e-05
EPS_UNIT = 1e-06

D = 512
ROWS, COLS = 8, 64
WINS = COLS // WIN + 1
CELLS = 24
OWN = 16
PATCHES = 4 * CELLS
TOKENS = WINS * PATCHES
ALL_CELLS = WINS * CELLS
OWN_CELLS = WINS * OWN
LANES = 128
VMEM_BYTES = 48 * 1024 * 1024

AXES = ("xl", "xh", "z", "y", "c")
CHIP_AXES = ("xl", "xh", "z", "y")
LON = ("xh", "z", "y", "c")

F32 = jnp.float32
BF16 = jnp.bfloat16


def device_index(x, y, z, c):
    return ((((x % 2) * 2 + x // 2) * 4 + z) * 4 + y) * 2 + c


def move(value, x=0, y=0, z=0, c=0):
    pairs = []
    for px in range(4):
        for pz in range(4):
            for py in range(4):
                for pc in range(2):
                    target = ((px + x) % 4, (py + y) % 4, (pz + z) % 4, (pc + c) % 2)
                    pairs.append((device_index(px, py, pz, pc), device_index(*target)))
    return lax.ppermute(value, AXES, pairs)


def slide(value, lat, lon):
    pairs = []
    for row in range(2):
        for col in range(64):
            pairs.append((row * 64 + col, (row + lat) % 2 * 64 + (col + lon) % 64))
    return lax.ppermute(value, AXES, pairs)


def half_of(value, which):
    width = value.shape[-1] // 2
    return lax.dynamic_slice_in_dim(value, which * width, width, value.ndim - 1)


def join_cores(mine, other, core, axis):
    return jnp.where(
        core == 0,
        jnp.concatenate([mine, other], axis=axis),
        jnp.concatenate([other, mine], axis=axis),
    )


def add_blocks(blocks):
    return jnp.sum(blocks.astype(F32), axis=0)


def own_rows(block, core):
    rows = block.shape[0] // 2
    mine = lax.dynamic_slice_in_dim(block, core * rows, rows, 0)
    other = move(lax.dynamic_slice_in_dim(block, (1 - core) * rows, rows, 0), c=1)
    return join_cores(mine, other, core, 1)


def inner(left, right):
    return lax.dot_general(left, right, (((0,), (0,)), ((), ())), preferred_element_type=F32)


def rims(fields, lat, before):
    near = [lax.dynamic_slice_in_dim(field, (1 - lat) * SHIFT, SHIFT, 0) for field in fields]
    across = slide(jnp.concatenate(near, axis=-1), 1, 0)
    *fields, before = lax.optimization_barrier((*fields, before))

    def cut(start):
        parts = [field[:, start : start + SHIFT].reshape(-1, field.shape[-1]) for field in fields]
        return jnp.concatenate(parts, axis=-1)

    west, east = slide(cut(COLS - SHIFT), 0, 1), slide(cut(0), 0, -1)
    count = SHIFT * SHIFT
    passed = [lax.dynamic_slice_in_dim(side, (1 - lat) * count, count, 0) for side in (west, east)]
    corners = slide(jnp.concatenate(passed, axis=0), 1, 0)
    return [across, west, east, corners], before


def dot(left, right):
    return jnp.dot(left, right, preferred_element_type=F32)


def dot_t(left, right):
    return lax.dot_general(left, right, (((1,), (1,)), ((), ())), preferred_element_type=F32)


def lay_out(wide, own, across, west, east, corners, groups, skipped=0):
    far = corners[...].astype(F32)
    sides = [
        (0, west[...].astype(F32), far[: SHIFT * SHIFT]),
        (SHIFT + COLS, east[...].astype(F32), far[SHIFT * SHIFT :]),
    ]
    for group in range(groups):
        lanes = slice(group * LANES, (group + 1) * LANES)
        rim_lanes = slice(skipped + group * LANES, skipped + (group + 1) * LANES)
        for row in range(ROWS + SHIFT):
            centre = own[row, :, lanes] if row < ROWS else across[row - ROWS, :, rim_lanes]
            wide[group, row, SHIFT : SHIFT + COLS, :] = centre.astype(F32)
            for start, close, corner in sides:
                part, at = (close, row) if row < ROWS else (corner, row - ROWS)
                wide[group, row, start : start + SHIFT, :] = part[SHIFT * at : SHIFT * (at + 1), rim_lanes]


def chunks(row_pairs):
    for win in range(WINS):
        for pair in range(row_pairs):
            for parity in range(4):
                row = 2 * pair + parity // 2
                yield win, pair, parity, row, pl.ds(WIN * win + parity % 2, 4, stride=2)


def give_back(out, wide):
    for group in range(4):
        lanes = slice(group * LANES, (group + 1) * LANES)
        for row in range(ROWS):
            out[row, :, lanes] = wide[group, row, SHIFT : SHIFT + COLS, :].astype(BF16)


def own_mask(per_window, shape):
    index = lax.broadcasted_iota(jnp.int32, shape, 0)
    win = index // per_window
    cell = (index % per_window) % (CELLS if per_window % CELLS == 0 else OWN)
    west = (win == 0) & (cell % 4 < 2)
    east = (win == WINS - 1) & (cell % 4 >= 2)
    return ((cell < OWN) & ~west & ~east).astype(F32)


def head_sums(values):
    row = lax.broadcasted_iota(jnp.int32, (D, D), 0) // 64
    col = lax.broadcasted_iota(jnp.int32, (D, D), 1) // 64
    same = (row == col).astype(BF16)
    high = values.astype(BF16)
    low = (values - high.astype(F32)).astype(BF16)
    return dot(high, same) + dot(low, same)


def normalize(values):
    centre = values - jnp.mean(values, axis=-1, keepdims=True)
    scale = lax.rsqrt(jnp.mean(centre * centre, axis=-1, keepdims=True) + EPS_NORM)
    return centre * scale, scale


def normalize_back(grad, normed, scale):
    mean = jnp.mean(grad, axis=-1, keepdims=True)
    slope = jnp.mean(grad * normed, axis=-1, keepdims=True)
    return scale * (grad - mean - normed * slope)


def lane_halves():
    lane = lax.broadcasted_iota(jnp.int32, (1, LANES), 1)
    return [(lane < 64).astype(BF16), (lane >= 64).astype(BF16)]


def fine_forward_kernel(
    spot, logit, own, across, west, east, corners, table, w_qkv, w_out,
    skip, merged_norm, merged_spread, normed, spread, units, unit_scale, weights, attended,
    wide, embedded,
):
    lay_out(wide, own, across, west, east, corners, 5)
    for win, pair, parity, row, cols in chunks(6):
        at = win * PATCHES + parity * CELLS + pair * 4
        for group in range(5):
            embedded[at : at + 4, group * LANES : (group + 1) * LANES] = wide[group, row, cols, :]

    @pl.loop(0, WINS)
    def _(win):
        rows = pl.ds(pl.multiple_of(win * PATCHES, 32), PATCHES)
        kind = embedded[rows, D : D + 1]
        first, second, third = table[0:1, :], table[1:2, :], table[2:3, :]
        added = jnp.where(kind == 0.0, first, jnp.where(kind == 1.0, second, third))
        values = embedded[rows, :D] + added
        embedded[rows, :D] = values
        unit, scale = normalize(values)
        normed[rows, :] = unit.astype(BF16)
        spread[rows, :] = scale

    block = TOKENS // 3
    for part in range(3):
        columns = slice(part * D, (part + 1) * D)
        for start in range(0, TOKENS, block):
            rows = slice(start, start + block)
            values = dot(normed[rows, :], w_qkv[:, columns])
            if part < 2:
                scale = lax.rsqrt(head_sums(values * values) + EPS_UNIT)
                unit_scale[rows, columns] = scale
                values = values * scale
            units[rows, columns] = values.astype(BF16)

    halves = lane_halves()
    outer = []
    for axis in range(2):
        index = lax.broadcasted_iota(jnp.int32, (PATCHES, PATCHES), axis)
        outer.append(((index % CELLS) // 8 == spot[0]).astype(jnp.int32))
    same = outer[0] == outer[1]

    @pl.loop(0, WINS)
    def _(win):
        rows = pl.ds(pl.multiple_of(win * PATCHES, 32), PATCHES)
        for duo in range(4):
            lanes = slice(duo * LANES, (duo + 1) * LANES)
            queries = units[rows, lanes]
            keys = units[rows, D + duo * LANES : D + (duo + 1) * LANES]
            values = units[rows, 2 * D + duo * LANES : 2 * D + (duo + 1) * LANES]
            total = jnp.zeros((PATCHES, LANES), F32)
            for side in range(2):
                head = 2 * duo + side
                scores = dot_t(queries, keys * halves[side]) * logit[head]
                exponent = jnp.where(same, jnp.exp(scores), 0.0)
                share = exponent * (1.0 / jnp.sum(exponent, axis=-1, keepdims=True))
                share = share.astype(BF16)
                weights[win * HEADS + head] = share
                total = total + dot(share, values * halves[side])
            attended[rows, lanes] = total.astype(BF16)

    for start in range(0, TOKENS, block):
        rows = slice(start, start + block)
        projected = dot(attended[rows, :], w_out[...]).astype(BF16).astype(F32)
        embedded[rows, :D] = (embedded[rows, :D] + projected).astype(BF16).astype(F32)
    for win in range(WINS):
        for parity in range(4):
            at = win * PATCHES + parity * CELLS
            skip[win * CELLS : (win + 1) * CELLS, parity * D : (parity + 1) * D] = embedded[
                at : at + CELLS, :D
            ]
    unit, scale = normalize(skip[...])
    merged_norm[...] = unit.astype(BF16)
    merged_spread[...] = scale


def spread_kernel(block, copies):
    for chip in range(64):
        copies[chip] = block[...]


def cotangent_kernel(own, across, west, east, corners, merged, rounded, wide):
    lay_out(wide, own, across, west, east, corners, 4, D + LANES)
    for win, pair, parity, row, cols in chunks(6):
        at = win * CELLS + pair * 4
        for group in range(4):
            lane = parity * D + group * LANES
            merged[at : at + 4, lane : lane + LANES] = wide[group, row, cols, :]
    rounded[...] = merged[...].astype(BF16)


def coarse_kernel(
    norm, norm_other, cot, cot_other, parts,
    coarse, grad_pre, split, blocks,
    merge, packed, sems,
):
    load_merge = pltpu.make_async_copy(parts.at[:, :32], merge, sems.at[0])
    load_split = pltpu.make_async_copy(parts.at[:, 32:], packed, sems.at[1])
    load_split.start()
    load_merge.start()
    load_split.wait()
    for j in range(2):
        pair = packed[:, 16 * j : 16 * j + 16, :].astype(F32)
        for k in range(2):
            quarter = pair[:, 8 * k : 8 * k + 8, :].reshape(512, 512)
            column = (2 * j + k) * 512
            split[:, column : column + 512] = quarter.astype(BF16)
    load_merge.wait()
    w_merge = merge[...].reshape(2048, 512)
    slope = 0.7978845608028654
    cubic = 0.044715
    keep = own_mask(CELLS, (ALL_CELLS, 1))
    own_grads, own_cots = [], []
    for i, (unit, cotangent) in enumerate(((norm, cot), (norm_other, cot_other))):
        value = dot(unit[...], w_merge)
        square = value * value
        bend = jnp.tanh(slope * (value + cubic * (square * value)))
        half_bend = 0.5 * (1.0 + bend)
        coarse[i] = (value * half_bend).astype(BF16)
        rise = half_bend + 0.5 * value * (1.0 - bend * bend) * slope * (1.0 + 3.0 * cubic * square)
        grad = dot_t(cotangent[...], split[...]) * rise
        grad_pre[i] = grad.astype(BF16)
        own_grads.append((grad * keep).astype(BF16))
        own_cots.append((coarse[i].astype(F32) * keep).astype(BF16))
    for x in range(4):
        chips = slice(x * 16, (x + 1) * 16)
        lanes = slice(x * 512, (x + 1) * 512)
        block = inner(norm[:, lanes], own_grads[0]) + inner(norm_other[:, lanes], own_grads[1])
        blocks[chips, :32, :] = block.astype(BF16).reshape(16, 32, 512)
    for j in range(2):
        quarters = []
        for k in range(2):
            lanes = slice((2 * j + k) * 512, (2 * j + k + 1) * 512)
            block = inner(own_cots[0], cot[:, lanes]) + inner(own_cots[1], cot_other[:, lanes])
            quarters.append(block.reshape(64, 8, 512))
        pair = jnp.concatenate(quarters, axis=1).astype(BF16)
        blocks[:, 32 + 16 * j : 48 + 16 * j, :] = pair


def partial_kernel(
    parts, coarse, grad_pre, split, grad_mine, grad_other, out_mine, out_other, merge, sem
):
    copy = pltpu.make_async_copy(parts.at[:, :32], merge, sem)
    copy.start()
    for i, out in enumerate((out_mine, out_other)):
        out[...] = dot(coarse[i], split[...]).astype(out.dtype)
    copy.wait()
    w_merge = merge[...].reshape(2048, 512)
    for i, out in enumerate((grad_mine, grad_other)):
        out[...] = dot_t(grad_pre[i], w_merge).astype(out.dtype)


def decode_kernel(skip, out_mine, received, decoded, sum_m, wide):
    sum_m[...] = skip[...] + out_mine[...] + received[...].astype(F32)
    for win, pair, parity, row, cols in chunks(4):
        at = win * CELLS + pair * 4
        for group in range(4):
            lane = parity * D + group * LANES
            wide[group, row, cols, :] = sum_m[at : at + 4, lane : lane + LANES]
    give_back(decoded, wide)


def fine_backward_kernel(
    spot, logit, grad_mine, received, cot, merged_norm, merged_spread,
    units, unit_scale, weights, normed, attended, w_out,
    grad_skip, grad_packed, grads_mine, grads_other,
    grad_tokens, grad_att, grad_units,
):
    grad = (grad_mine[...] + received[...].astype(F32)).astype(BF16).astype(F32)
    grad_skip[...] = cot[...] + normalize_back(grad, merged_norm[...].astype(F32), merged_spread[...])
    for win in range(WINS):
        for parity in range(4):
            at = win * PATCHES + parity * CELLS
            grad_tokens[at : at + CELLS, :] = grad_skip[
                win * CELLS : (win + 1) * CELLS, parity * D : (parity + 1) * D
            ]
    block = TOKENS // 3
    for start in range(0, TOKENS, block):
        rows = slice(start, start + block)
        grad_att[rows, :] = dot_t(grad_tokens[rows, :].astype(BF16), w_out[...]).astype(BF16)
    halves = lane_halves()

    @pl.loop(0, WINS)
    def _(win):
        rows = pl.ds(pl.multiple_of(win * PATCHES, 32), PATCHES)
        for duo in range(4):
            lanes = slice(duo * LANES, (duo + 1) * LANES)
            key_lanes = slice(D + duo * LANES, D + (duo + 1) * LANES)
            value_lanes = slice(2 * D + duo * LANES, 2 * D + (duo + 1) * LANES)
            queries, keys, values = units[rows, lanes], units[rows, key_lanes], units[rows, value_lanes]
            grad_out = grad_att[rows, lanes]
            grad_q = jnp.zeros((PATCHES, LANES), F32)
            grad_k = jnp.zeros((PATCHES, LANES), F32)
            grad_v = jnp.zeros((PATCHES, LANES), F32)
            for side in range(2):
                head = 2 * duo + side
                half = halves[side]
                share = weights[win * HEADS + head]
                wide_share = share.astype(F32)
                flow = dot_t(grad_out, values * half) * wide_share
                flow = flow - wide_share * jnp.sum(flow, axis=-1, keepdims=True)
                flow = (flow * logit[head]).astype(BF16)
                grad_q = grad_q + dot(flow, keys * half)
                grad_k = grad_k + inner(flow, queries * half)
                grad_v = grad_v + inner(share, grad_out * half)
            grad_units[rows, lanes] = grad_q
            grad_units[rows, key_lanes] = grad_k
            grad_packed[rows, value_lanes] = grad_v.astype(BF16)

    for part in range(2):
        columns = slice(part * D, (part + 1) * D)
        for start in range(0, TOKENS, block):
            rows = slice(start, start + block)
            unit = units[rows, columns].astype(F32)
            grad = grad_units[rows, columns]
            along = head_sums(unit * grad)
            grad_packed[rows, columns] = (
                unit_scale[rows, columns] * (grad - unit * along)
            ).astype(BF16)
    keep = own_mask(PATCHES, (TOKENS, 1))
    own_grad = (grad_tokens[...] * keep).astype(BF16)
    own_normed = (normed[...].astype(F32) * keep).astype(BF16)
    for part in range(4):
        if part < 3:
            result = inner(own_normed, grad_packed[:, part * D : (part + 1) * D]).astype(BF16)
        else:
            result = inner(attended[...], own_grad).astype(BF16)
        lanes = slice(part % 2 * D, (part % 2 + 1) * D)

        @pl.when(spot[1] == part // 2)
        def _():
            grads_mine[:, lanes] = result

        @pl.when(spot[1] != part // 2)
        def _():
            grads_other[:, lanes] = result


def field_grad_kernel(grad_skip, grad_packed, normed, spread, w_qkv, grad_fields, total, wide):
    block = TOKENS // 3
    for start in range(0, TOKENS, block):
        rows = slice(start, start + block)
        grad = dot_t(grad_packed[rows, :], w_qkv[...]).astype(BF16).astype(F32)
        total[rows, :] = normalize_back(grad, normed[rows, :].astype(F32), spread[rows, :])
    for win, pair, parity, row, cols in chunks(4):
        at = win * PATCHES + parity * CELLS + pair * 4
        cell = win * CELLS + pair * 4
        for group in range(4):
            lanes = slice(group * LANES, (group + 1) * LANES)
            lane = parity * D + group * LANES
            wide[group, row, cols, :] = (
                total[at : at + 4, lanes] + grad_skip[cell : cell + 4, lane : lane + LANES]
            )
    give_back(grad_fields, wide)


def kernel_call(
    kernel, name, outs, scratch, args, scalars=0, ahead=0, in_place=0, flops=0, moved=0
):
    count = len(args)
    specs = []
    for index in range(count):
        if index < scalars:
            specs.append(pl.BlockSpec(memory_space=pltpu.SMEM))
        elif index < ahead or index >= count - in_place:
            specs.append(pl.BlockSpec(memory_space=pl.ANY))
        else:
            specs.append(pl.BlockSpec(memory_space=pltpu.VMEM))
    shapes = [jax.ShapeDtypeStruct(shape, dtype) for shape, dtype in outs]
    return pl.pallas_call(
        kernel,
        out_shape=shapes,
        in_specs=specs,
        out_specs=[pl.BlockSpec(memory_space=pltpu.VMEM)] * len(outs),
        scratch_shapes=scratch,
        compiler_params=pltpu.CompilerParams(vmem_limit_bytes=VMEM_BYTES),
        cost_estimate=pl.CostEstimate(flops=flops, bytes_accessed=moved, transcendentals=0),
        name=name,
    )(*args)


def per_device(
    fields, surface, surface_table, logit_scale, w_qkv, w_out, w_merge, w_split, cotangent
):
    core = lax.axis_index("c")
    lat = lax.axis_index("xl")
    spot = jnp.stack([lat, core]).astype(jnp.int32)
    kinds = jnp.broadcast_to(surface.astype(BF16)[:, :, None], (ROWS, COLS, LANES))
    own_fields = jnp.concatenate([fields, kinds], axis=-1)

    index = jnp.arange(1024, dtype=jnp.int32)
    source = index % 512 // 8 * 16 + index // 512 * 8 + index % 8
    runs = (index[:, None] == source[None, :]).astype(BF16)
    sorted_merge = jnp.dot(w_merge, runs, preferred_element_type=F32).astype(BF16)
    far = move(half_of(sorted_merge, 1 - core), c=1)
    rim, far = rims((fields, kinds, cotangent), lat, far)
    merge_block = join_cores(half_of(sorted_merge, core), far, core, 0)
    split_block = w_split.reshape(8, 4, 512).transpose(1, 0, 2).reshape(32, 512)
    block = jnp.concatenate([merge_block, split_block], axis=0)
    (copies,) = kernel_call(
        spread_kernel, "spread_weights", [((64, 64, 512), BF16)], [], (block,), moved=4_000_000
    )
    *rim, copies = lax.optimization_barrier((*rim, copies))
    mine = lax.all_to_all(copies, CHIP_AXES, 0, 0, tiled=True)

    cells = (ALL_CELLS, 4 * D)
    skip, merged_norm, merged_spread, normed, spread, units, unit_scale, weights, attended = kernel_call(
        fine_forward_kernel,
        "fine_forward",
        [
            (cells, F32),
            (cells, BF16),
            ((ALL_CELLS, 1), F32),
            ((TOKENS, D), BF16),
            ((TOKENS, 1), F32),
            ((TOKENS, 3 * D), BF16),
            ((TOKENS, 2 * D), F32),
            ((WINS * HEADS, PATCHES, PATCHES), BF16),
            ((TOKENS, D), BF16),
        ],
        [pltpu.VMEM((5, 12, 72, LANES), F32), pltpu.VMEM((TOKENS, D + LANES), F32)],
        (spot, logit_scale, own_fields, *rim, surface_table, w_qkv, w_out),
        scalars=2,
        flops=15_000_000_000,
        moved=12_000_000,
    )
    cot, cot_rounded = kernel_call(
        cotangent_kernel,
        "cotangent_cells",
        [(cells, F32), (cells, BF16)],
        [pltpu.VMEM((4, 12, 72, LANES), F32)],
        (cotangent, *rim),
        moved=8_000_000,
    )
    norm_other, cot_other = move(merged_norm, c=1), move(cot_rounded, c=1)
    merged_spread, mine = lax.optimization_barrier((merged_spread, mine))
    coarse, grad_pre, split, blocks = kernel_call(
        coarse_kernel,
        "coarse",
        [
            ((2, ALL_CELLS, 512), BF16),
            ((2, ALL_CELLS, 512), BF16),
            ((512, 2048), BF16),
            ((64, 64, 512), BF16),
        ],
        [
            pltpu.VMEM((64, 32, 512), BF16),
            pltpu.VMEM((64, 32, 512), BF16),
            pltpu.SemaphoreType.DMA((2,)),
        ],
        (merged_norm, norm_other, cot_rounded, cot_other, mine),
        in_place=1,
        flops=8_000_000_000,
        moved=15_000_000,
    )
    split, blocks = lax.optimization_barrier((split, blocks))
    blocks = lax.all_to_all(blocks, CHIP_AXES, 0, 0, tiled=True)
    grad_mine, grad_other, out_mine, out_other = kernel_call(
        partial_kernel,
        "partial_products",
        [(cells, F32), (cells, BF16), (cells, F32), (cells, BF16)],
        [pltpu.VMEM((64, 32, 512), BF16), pltpu.SemaphoreType.DMA],
        (mine, coarse, grad_pre, split),
        ahead=1,
        flops=3_000_000_000,
        moved=10_000_000,
    )
    grad_skip, grad_packed, fine_mine, fine_other = kernel_call(
        fine_backward_kernel,
        "fine_backward",
        [(cells, F32), ((TOKENS, 3 * D), BF16), ((D, 1024), BF16), ((D, 1024), BF16)],
        [
            pltpu.VMEM((TOKENS, D), F32),
            pltpu.VMEM((TOKENS, D), BF16),
            pltpu.VMEM((TOKENS, 2 * D), F32),
        ],
        (
            spot,
            logit_scale,
            grad_mine,
            move(grad_other, c=1),
            cot,
            merged_norm,
            merged_spread,
            units,
            unit_scale,
            weights,
            normed,
            attended,
            w_out,
        ),
        scalars=2,
        flops=15_000_000_000,
        moved=15_000_000,
    )
    (decoded,) = kernel_call(
        decode_kernel,
        "decode",
        [((ROWS, COLS, D), BF16)],
        [pltpu.VMEM(cells, F32), pltpu.VMEM((4, 8, 72, LANES), F32)],
        (skip, out_mine, move(out_other, c=1)),
        moved=8_000_000,
    )
    (grad_fields,) = kernel_call(
        field_grad_kernel,
        "field_grad",
        [((ROWS, COLS, D), BF16)],
        [pltpu.VMEM((TOKENS, D), F32), pltpu.VMEM((4, 8, 72, LANES), F32)],
        (grad_skip, grad_packed, normed, spread, w_qkv),
        flops=4_000_000_000,
        moved=8_000_000,
    )
    fine_half = (fine_mine.astype(F32) + move(fine_other, c=1).astype(F32)).astype(BF16)
    fine_half, blocks = lax.optimization_barrier((fine_half, blocks))
    fine_blocks = lax.all_to_all(fine_half.reshape(64, D // 64, 1024), CHIP_AXES, 0, 0, tiled=True)
    fine_sum = add_blocks(fine_blocks)
    fine_own = lax.dynamic_slice_in_dim(fine_sum, core * 4, 4, 0)
    fine_far = move(lax.dynamic_slice_in_dim(fine_sum, (1 - core) * 4, 4, 0), c=1)
    first, second = jnp.where(core == 0, fine_own, fine_far), jnp.where(core == 0, fine_far, fine_own)
    blocks = add_blocks(blocks)
    grad_split = blocks[32:].reshape(4, 8, 512).transpose(1, 0, 2).reshape(8, 2048)
    grad_merge = own_rows(blocks[:32], core).reshape(16, 2, 64, 8).transpose(0, 2, 1, 3)
    return (
        decoded,
        grad_fields,
        jnp.concatenate([first, second[:, :D]], axis=1),
        second[:, D:],
        grad_merge.reshape(16, 1024),
        grad_split,
    )


def solution(mesh):
    fine_mesh = Mesh(mesh.devices.reshape(2, 2, 4, 4, 2), AXES)
    grid, rows = P("xl", LON, None), P(AXES, None)
    in_specs = (grid, P("xl", LON), P(), P(), P(), P(), rows, rows, grid)
    out_specs = (grid, grid, rows, rows, rows, rows)
    return jax.shard_map(
        per_device, mesh=fine_mesh, in_specs=in_specs, out_specs=out_specs, check_vma=False
    )
```
